256 devices in a mesh: dp: 16 (over y, x), ctx: 16 (over z, core).
Axes of the slice: x: 4, y: 4, z: 8, core: 2. Of those that a mesh axis runs over, the one named last changes fastest.
Arguments:
- queries: bfloat16 [32768, 12288], P(('dp', 'ctx')), may hold values from -8 to 8
- latent: bfloat16 [32768, 576], P(('dp', 'ctx')), may hold values from -8 to 8
- w_kv: bfloat16 [512, 16384], P(None, 'ctx'), may hold values from -0.25 to 0.25
- grad_out: bfloat16 [32768, 8192], P(('dp', 'ctx')), may hold values from -6 to 6
- doc_lengths: int32 [16, 16], replicated, may hold values from 1 to 256, 2048 in all within a row
- matching: int32 [16], replicated, may hold values from 0 to 15, each once
Outputs:
- grad_queries: bfloat16 [32768, 12288], P(('dp', 'ctx'))
- grad_latent: float32 [32768, 576], P(('dp', 'ctx'))
- grad_weight: float32 [512, 16384], P('dp', 'ctx')
The draws below stay inside these ranges and needn't reach their ends.
Inputs may be any that keep to these rules, and one draw needn't show every extreme that they name: `doc_lengths`: each row sums to 2048, and its largest length is 256. `matching`: a permutation of the packs.
All inputs are finite; a program needn't handle non-finite values.
Results may differ from the reference program's by a relative error of at most 0.013.
Values may be sent and summed in bfloat16 or wider, within the bound.
A program may use at most 128 MiB of HBM per device.

```python
import math
import jax
import jax.numpy as jnp
import numpy as np
from jax import lax

HEADS = 64
NOPE = 128
ROPE = 64
VDIM = 128
LATENT = 512
QBLK = 256
MOST = 256
PACK = 2048
TOKENS = 32768
DOCS = 16
N_DP = 16


def draw_queries(key, part):
    key = jax.random.fold_in(key, 1)
    column_count = HEADS * (NOPE + ROPE)
    return jax.random.truncated_normal(key, -4.0, 4.0, (TOKENS, column_count), jnp.float32).astype(jnp.bfloat16)


def draw_latent(key, part):
    key = jax.random.fold_in(key, 2)
    column_count = LATENT + ROPE
    return jax.random.truncated_normal(key, -4.0, 4.0, (TOKENS, column_count), jnp.float32).astype(jnp.bfloat16)


def steps_of(own_key, dims, shards, low, top_value):
    loudness = 1.0
    for axis_at, blocks in shards:
        heights = jax.random.uniform(jax.random.fold_in(jax.random.fold_in(own_key, 6), axis_at), (blocks,), jnp.float32, low / len(shards), top_value / len(shards))
        loudness = loudness * jnp.repeat(jnp.exp(heights), dims[axis_at] // blocks).reshape((-1,) + (1,) * (len(dims) - 1 - axis_at))
    return loudness


def profile(count, total, limit, skew):
    portions = [(1 << 20) // math.isqrt(standing ** skew) + 1 for standing in range(2, count + 1)]
    surplus, given = total - limit - (count - 1), [1] * (count - 1)
    while surplus > 0:
        free = [i for i in range(count - 1) if given[i] < limit]
        pool, left = sum([portions[i] for i in free]), surplus
        for i in free:
            more = min(limit - given[i], max(1, left * portions[i] // pool), surplus)
            given[i] = given[i] + more
            surplus = surplus - more
    return np.array([limit] + given)


def uneven(key, amount, total, limit, slope):
    if amount == 2:
        one = jax.random.randint(key, (), max(1, total - limit), min(limit, total - 1) + 1)
        return jnp.stack([one, total - one])
    tallies = jnp.asarray(profile(amount, total, limit, slope), jnp.int32)
    twos = (amount - 1) // 2
    giver, receiver = tallies[1:1 + 2 * twos:2], tallies[2:2 + 2 * twos:2]
    room = jnp.minimum(giver - 1, limit - receiver)
    shifted = jax.random.randint(jax.random.fold_in(key, 1), (twos,), 0, 1 << 20) % (room + 1)
    tallies = tallies.at[1:1 + 2 * twos:2].set(giver - shifted).at[2:2 + 2 * twos:2].set(receiver + shifted)
    return tallies[jax.random.permutation(jax.random.fold_in(key, 2), amount)]


def scatter_about(rng, shape, deviation, reach, cuts=(), held_as=jnp.bfloat16):
    values = jax.random.normal(rng, shape, jnp.float32) * deviation
    if len(cuts) > 0:
        values = steps_of(rng, shape, cuts, -0.22, 0.18) * values
    return jnp.clip(values, min=-reach, max=reach).astype(held_as)


def setup_inputs(seed: int = 0) -> dict:
    splits = jax.random.split(jax.random.key(seed), 7)
    return {
        "queries": draw_queries(jax.random.fold_in(splits[6], 71), 0),
        "latent": draw_latent(jax.random.fold_in(splits[6], 71), 0),
        "w_kv": scatter_about(splits[2], (LATENT, HEADS * (NOPE + VDIM)), LATENT ** -0.5, 0.25, ((1, 16),)),
        "grad_out": scatter_about(splits[3], (TOKENS, HEADS * VDIM), 1.0, 6.0, ((0, 256),)),
        "doc_lengths": jax.vmap(lambda own: uneven(own, DOCS, PACK, MOST, 2))(jax.random.split(splits[4], N_DP)).reshape((N_DP, DOCS)).astype(jnp.int32),
        "matching": jax.random.permutation(splits[5], N_DP).astype(jnp.int32),
    }


def windowed(values_in, count_of_blocks):
    split_rows = values_in.reshape(count_of_blocks, QBLK, values_in.shape[-1])
    earlier = jnp.concatenate([jnp.zeros_like(split_rows[:1]), split_rows[:-1]], axis=0)[:, QBLK - MOST:]
    return jnp.concatenate([earlier, split_rows], axis=1)


def restore_from_span(window_grad, count_of_blocks, sequence_length):
    tail_part = window_grad[:, :MOST]
    own_part = window_grad[:, MOST:]
    padding = jnp.zeros((count_of_blocks, QBLK - MOST, window_grad.shape[-1]), jnp.float32)
    spilled = jnp.concatenate([padding, tail_part], axis=1)
    moved = jnp.concatenate([spilled[1:], jnp.zeros_like(spilled[:1])], axis=0)
    return (own_part + moved).reshape(sequence_length, window_grad.shape[-1])


def head_grads(query_rows, kv_rows, rope_rows, grad_rows, segment):
    sequence_length = query_rows.shape[0]
    count_of_blocks = sequence_length // QBLK
    logit_scale = float(NOPE + ROPE) ** -0.5
    key_rows = jnp.concatenate([kv_rows[:, :NOPE], rope_rows], axis=1)
    value_rows = kv_rows[:, NOPE:]
    blocked_queries = query_rows.reshape(count_of_blocks, QBLK, -1).astype(jnp.float32)
    key_span_rows = windowed(key_rows, count_of_blocks).astype(jnp.float32)
    value_span_rows = windowed(value_rows, count_of_blocks).astype(jnp.float32)
    block_gradients = grad_rows.reshape(count_of_blocks, QBLK, -1).astype(jnp.float32)
    seg_query = segment.reshape(count_of_blocks, QBLK)
    seg_key = windowed(segment[:, None], count_of_blocks)[:, :, 0]
    query_place = jnp.arange(sequence_length, dtype=jnp.int32).reshape(count_of_blocks, QBLK)
    key_place = query_place[:, :1] - MOST + jnp.arange(QBLK + MOST, dtype=jnp.int32)[None, :]
    allowed = (key_place[:, None, :] >= 0) & (key_place[:, None, :] <= query_place[:, :, None]) & (seg_key[:, None, :] == seg_query[:, :, None])
    logit_matrix = jnp.einsum("roj,rmj->rom", blocked_queries, key_span_rows) * logit_scale
    logit_matrix = jnp.where(allowed, logit_matrix, -jnp.inf)
    attn_weights = jax.nn.softmax(logit_matrix, axis=-1)
    reduced_precision_weights = attn_weights.astype(jnp.bfloat16)
    attention_output = jnp.einsum("yge,yel->ygl", reduced_precision_weights.astype(jnp.float32), value_span_rows)
    row_dot = jnp.sum(block_gradients * attention_output, axis=-1, keepdims=True)
    probability_gradient = jnp.einsum("roj,rmj->rom", block_gradients, value_span_rows)
    score_gradient = (attn_weights * (probability_gradient - row_dot)).astype(jnp.bfloat16).astype(jnp.float32)
    query_gradient = jnp.einsum("yge,yel->ygl", score_gradient, key_span_rows) * logit_scale
    key_gradient = restore_from_span(jnp.einsum("fle,flg->feg", score_gradient, blocked_queries) * logit_scale, count_of_blocks, sequence_length)
    value_gradient = restore_from_span(jnp.einsum("fle,flg->feg", reduced_precision_weights.astype(jnp.float32), block_gradients), count_of_blocks, sequence_length)
    grad_kv_head = jnp.concatenate([key_gradient[:, :NOPE], value_gradient], axis=1)
    return query_gradient.reshape(sequence_length, -1), grad_kv_head, key_gradient[:, NOPE:]


def reference(queries, latent, w_kv, grad_out, doc_lengths, matching):
    width_qk = NOPE + ROPE
    width_kv = NOPE + VDIM

    def one_group(total_weight, group):
        source = matching[group]
        first_row = (source * PACK).astype(jnp.int32)
        query_pack = lax.dynamic_slice_in_dim(queries, first_row, PACK, 0)
        latent_pack = lax.dynamic_slice_in_dim(latent, first_row, PACK, 0)
        grad_pack = lax.dynamic_slice_in_dim(grad_out, first_row, PACK, 0)
        doc_ends = jnp.cumsum(doc_lengths[source]).astype(jnp.int32)
        token_place = jnp.arange(PACK, dtype=jnp.int32)
        segment = jnp.sum((token_place[:, None] >= doc_ends[None, :]).astype(jnp.int32), axis=1)
        key_values = jnp.dot(latent_pack[:, :LATENT], w_kv, preferred_element_type=jnp.float32).astype(jnp.bfloat16)
        rope_rows = latent_pack[:, LATENT:]
        query_heads = query_pack.reshape(PACK, HEADS, width_qk).transpose(1, 0, 2)
        kv_heads = key_values.reshape(PACK, HEADS, width_kv).transpose(1, 0, 2)
        grad_heads = grad_pack.reshape(PACK, HEADS, VDIM).transpose(1, 0, 2)
        query_gradient, grad_kv_heads, grad_rope = lax.map(
            lambda pieces: head_grads(pieces[0], pieces[1], rope_rows, pieces[2], segment),
            (query_heads, kv_heads, grad_heads))
        grad_query_pack = query_gradient.transpose(1, 0, 2).reshape(PACK, HEADS * width_qk).astype(jnp.bfloat16)
        grad_kv = grad_kv_heads.transpose(1, 0, 2).reshape(PACK, HEADS * width_kv).astype(jnp.bfloat16)
        latent_nope = jnp.dot(grad_kv, w_kv.T, preferred_element_type=jnp.float32)
        latent_rope = jnp.sum(grad_rope, axis=0)
        grad_latent_pack = jnp.concatenate([latent_nope, latent_rope], axis=1)
        total_weight = total_weight + jnp.dot(latent_pack[:, :LATENT].T, grad_kv, preferred_element_type=jnp.float32)
        return total_weight, (grad_query_pack, grad_latent_pack)

    start_weight = jnp.zeros((LATENT, HEADS * width_kv), jnp.float32)
    grad_weight, (grad_query_all, grad_latent_all) = lax.scan(one_group, start_weight, jnp.arange(N_DP, dtype=jnp.int32))
    return (grad_query_all.reshape(TOKENS, HEADS * width_qk),
            grad_latent_all.reshape(TOKENS, LATENT + ROPE),
            grad_weight)
```

```python
import functools

import jax
import jax.numpy as jnp
from jax import lax
from jax.experimental import pallas as pl
from jax.experimental.pallas import tpu as pltpu
from jax.sharding import PartitionSpec as P

NOPE = 128
ROPE = 64
VDIM = 128
LATENT = 512
HEADS = 64
ROWS = 128
QK = NOPE + ROPE
KV = NOPE + VDIM
WIDE = LATENT + ROPE
MESH = pl.DeviceIdType.MESH
ANY = pl.BlockSpec(memory_space=pl.ANY)
BF = jnp.bfloat16
F32 = jnp.float32
LOW = -1e30


def place():
    dp, ctx = lax.axis_index("dp"), lax.axis_index("ctx")
    return dp // 4, lax.rem(dp, 4), ctx // 2, lax.rem(ctx, 2)


def pick(axis, on_x, on_y):
    return (1 - axis) * on_x + axis * on_y


def wrap(value, n):
    return lax.rem(value + n, n)


def line_dp(axis, position, y, x):
    return pick(axis, 4 * y + position, 4 * position + x)


class Sender:
    def __init__(self):
        self.sent = []
        self.due = []

    def remote(self, src, dst, send_sem, recv_sem, device):
        copy = pltpu.make_async_remote_copy(
            src_ref=src, dst_ref=dst, send_sem=send_sem, recv_sem=recv_sem,
            device_id=device, device_id_type=MESH,
        )
        copy.start()
        self.sent.append(copy)
        return copy

    def local(self, src, dst, sem):
        copy = pltpu.make_async_copy(src, dst, sem)
        copy.start()
        self.due.append(copy)

    def finish(self):
        for copy in self.due:
            copy.wait()
        for copy in self.sent:
            copy.wait_recv()
        for copy in self.sent:
            copy.wait_send()


def signal(device):
    pl.semaphore_signal(pltpu.get_barrier_semaphore(), inc=1, device_id=device, device_id_type=MESH)


def call(kernel, name, number, out_shape, semaphores):
    return pl.pallas_call(
        kernel,
        out_shape=out_shape,
        in_specs=None,
        out_specs=jax.tree.map(lambda _: ANY, out_shape),
        scratch_shapes=[pltpu.SemaphoreType.DMA(s) for s in semaphores],
        compiler_params=pltpu.CompilerParams(collective_id=number, has_side_effects=True),
        name=name,
    )


def gather_kernel(q, latent, w, g, q_out, g_out, lat_out, w_out, send, recv, w_send, w_recv, w_send2, w_recv2):
    y, x, z, core = place()
    dp = 4 * y + x
    mine = pick(core, x, y)
    other = pick(core, y, x)
    before, after = wrap(z - 1, 8), wrap(z + 1, 8)
    w_axis = z // 4
    w_match = (pick(w_axis, x, y) == lax.rem(z, 4)).astype(jnp.int32)
    w_other = pick(w_axis, y, x)
    same_core = (w_axis == core).astype(jnp.int32)
    w_chip = 4 * core + mine

    for e in range(2):
        half = lax.rem(core + e, 2)
        for d in range(4):
            source = line_dp(core, wrap(mine - d, 4), y, x)
            if d or e:
                signal((source, 2 * z + half))
            signal((source, 2 * before + half))
    for d in range(1, 4):
        signal((line_dp(1 - core, wrap(other - d, 4), y, x), 2 * z + core))
    for b in range(2):
        away = (w_chip != z) | (core != b)

        @pl.when(away)
        def _():
            signal((dp, 2 * w_chip + b))

    barrier = pltpu.get_barrier_semaphore()
    pl.semaphore_wait(barrier, 18 + w_match * (8 - same_core))

    moves = Sender()
    w_rows = w.at[pl.ds(pl.multiple_of(w_other * (LATENT // 4), LATENT // 4), LATENT // 4)]
    w_width = w.shape[1]

    def w_slot(quarter, b):
        return w_out.at[quarter, :, pl.ds(pl.multiple_of(b * w_width, w_width), w_width)]

    def w_copy(dz):
        target = (dp, 2 * lax.rem(z + dz, 8) + w_axis)
        return pltpu.make_async_remote_copy(
            src_ref=w_rows, dst_ref=w_slot(w_other, core), send_sem=w_send.at[dz], recv_sem=w_recv.at[core],
            device_id=target, device_id_type=MESH,
        )

    @pl.when(w_match == 1)
    def _():
        @pl.when(same_core == 1)
        def _():
            pltpu.make_async_copy(w_rows, w_slot(w_other, core), w_recv.at[core]).start()

        @pl.when(same_core == 0)
        def _():
            w_copy(0).start()

        for dz in (4, 1, 7, 2, 6, 3, 5):
            w_copy(dz).start()

    q_width = q.shape[1] // 8
    g_width = g.shape[1] // 8
    for e in range(2):
        axis = lax.rem(core + e, 2)
        spot = pick(axis, x, y)
        for d in range(4):
            target = line_dp(axis, lax.rem(spot + d, 4), y, x)
            k = 4 * e + d
            lat_own = lat_out.at[spot, 2 + core]
            if d == 0 and e == 0:
                moves.local(latent, lat_own, recv.at[2, k])
            else:
                moves.remote(latent, lat_own, send.at[2, k], recv.at[2, k], (target, 2 * z + axis))
            moves.remote(latent, lat_out.at[spot, core], send.at[3, k], recv.at[3, k], (target, 2 * after + axis))
    for d in (2, 1, 3, 0):
        for e in range(2):
            axis = lax.rem(core + e, 2)
            spot = pick(axis, x, y)
            there = lax.rem(spot + d, 4)
            target = (line_dp(axis, there, y, x), 2 * z + axis)
            k = 4 * e + d
            q_part = q.at[:, pl.ds(pl.multiple_of((4 * axis + there) * q_width, q_width), q_width)]
            g_part = g.at[:, pl.ds(pl.multiple_of((4 * axis + there) * g_width, g_width), g_width)]
            if d == 0 and e == 0:
                moves.local(q_part, q_out.at[spot, core], recv.at[0, k])
                moves.local(g_part, g_out.at[spot, core], recv.at[1, k])
            else:
                moves.remote(q_part, q_out.at[spot, core], send.at[0, k], recv.at[0, k], target)
                moves.remote(g_part, g_out.at[spot, core], send.at[1, k], recv.at[1, k], target)

    for b in range(2):
        slot = w_slot(other, b)
        pltpu.make_async_copy(slot, slot, w_recv.at[b]).wait()
    for d in range(1, 4):
        target = (line_dp(1 - core, lax.rem(other + d, 4), y, x), 2 * z + core)
        moves.remote(w_out.at[other], w_out.at[other], w_send2.at[d], w_recv2.at[d], target)
    moves.finish()

    @pl.when(w_match == 1)
    def _():
        @pl.when(same_core == 0)
        def _():
            w_copy(0).wait_send()

        for dz in range(1, 8):
            w_copy(dz).wait_send()


def gather(q, latent, w, g):
    rows = q.shape[0]
    shapes = [
        jax.ShapeDtypeStruct((4, 2, rows, q.shape[1] // 8), BF),
        jax.ShapeDtypeStruct((4, 2, rows, g.shape[1] // 8), BF),
        jax.ShapeDtypeStruct((4, 4, rows, latent.shape[1]), BF),
        jax.ShapeDtypeStruct((4, w.shape[0] // 4, 2 * w.shape[1]), BF),
    ]
    run = pl.pallas_call(
        gather_kernel,
        out_shape=shapes,
        in_specs=[ANY] * 4,
        out_specs=[ANY] * 4,
        scratch_shapes=[
            pltpu.SemaphoreType.DMA((4, 8)),
            pltpu.SemaphoreType.DMA((4, 8)),
            pltpu.SemaphoreType.DMA((8,)),
            pltpu.SemaphoreType.DMA((2,)),
            pltpu.SemaphoreType.DMA((4,)),
            pltpu.SemaphoreType.DMA((4,)),
        ],
        compiler_params=pltpu.CompilerParams(collective_id=0, has_side_effects=True),
        name="gather_inputs",
    )
    return run(q, latent, w, g)


def nt(a, b):
    return lax.dot_general(a, b, (((1,), (1,)), ((), ())), preferred_element_type=F32)


def tn(a, b):
    return lax.dot_general(a, b, (((0,), (0,)), ((), ())), preferred_element_type=F32)


def nn(a, b):
    return jnp.dot(a, b, preferred_element_type=F32)


def heads_kernel(lo, q, g, lat, w, gq, d_halo, d_own, dw, kv, gkv, p_t, ds_t, dw_sum, rope_sum):
    step = pl.program_id(0)
    rows = q.shape[2]
    block = 2 * rows
    window = 4 * rows
    scale = float(QK) ** -0.5
    pairs = gq.shape[1]
    part = 2 * KV

    @pl.when(step == 0)
    def _():
        p_t[...] = jnp.zeros_like(p_t)
        ds_t[...] = jnp.zeros_like(ds_t)
        dw_sum[...] = jnp.zeros_like(dw_sum)

    rope_sum[...] = jnp.zeros_like(rope_sum)
    nope = lat[0, :, :, :LATENT].reshape(window, LATENT)
    rope = lat[0, :, :, LATENT:].reshape(window, ROPE)
    lows = lo[0]
    key_at = lax.broadcasted_iota(jnp.int32, (3 * rows, rows), 0)
    query_at = lax.broadcasted_iota(jnp.int32, (3 * rows, rows), 1)

    def project(i, _):
        cols = pl.ds(pl.multiple_of(i * part, part), part)
        kv[:, cols] = nn(nope, w[:, cols]).astype(BF)
        return 0

    lax.fori_loop(0, pairs, project, 0)

    def pair(i, _):
        q_two = q[0, :, :, pl.ds(pl.multiple_of(i * 2 * QK, 2 * QK), 2 * QK)].reshape(block, 2 * QK)
        g_two = g[0, :, :, pl.ds(pl.multiple_of(i * 2 * VDIM, 2 * VDIM), 2 * VDIM)].reshape(block, 2 * VDIM)
        cols = pl.ds(pl.multiple_of(i * part, part), part)
        kv_two = kv[:, cols]
        dq_two, dkv_two = [], []
        for h in range(2):
            qh = q_two[:, h * QK:(h + 1) * QK]
            gh = g_two[:, h * VDIM:(h + 1) * VDIM]
            kh = jnp.concatenate([kv_two[:, h * KV:h * KV + NOPE], rope], axis=1)
            vh = kv_two[:, h * KV + NOPE:(h + 1) * KV]
            scores = nt(kh, qh)
            dprobs = nt(vh, gh)
            for s in range(2):
                keys = slice(rows * s, rows * s + 3 * rows)
                queries = slice(rows * s, rows * s + rows)
                low = lows[:, queries] - rows * s
                seen = (key_at >= low) & (key_at <= query_at + block)
                sc = jnp.where(seen, scores[keys, queries] * scale, LOW)
                top = jnp.max(sc, axis=0, keepdims=True)
                ex = jnp.exp(sc - top)
                probs = ex * (1.0 / jnp.sum(ex, axis=0, keepdims=True))
                probs_low = probs.astype(BF)
                dp = dprobs[keys, queries]
                row_dot = jnp.sum(probs_low.astype(F32) * dp, axis=0, keepdims=True)
                p_t[h, keys, queries] = probs_low
                ds_t[h, keys, queries] = (probs * (dp - row_dot)).astype(BF)
            ds = ds_t[h]
            dq_two.append((tn(ds, kh) * scale).astype(BF))
            dk = nn(ds, qh) * scale
            dv = nn(p_t[h], gh)
            rope_sum[...] += dk[:, NOPE:]
            dkv_two += [dk[:, :NOPE].astype(BF), dv.astype(BF)]
        gkv[:, cols] = jnp.concatenate(dkv_two, axis=1)
        gq[0, i] = jnp.concatenate(dq_two, axis=1).reshape(2, rows, 2 * QK)
        return 0

    lax.fori_loop(0, pairs, pair, 0)

    d_nope = nt(gkv[...], w[...]).astype(BF)
    d_rope = rope_sum[...].astype(BF)
    d_halo[0, :, :LATENT] = d_nope[:block]
    d_halo[0, :, LATENT:] = d_rope[:block]
    d_own[0, :, :LATENT] = d_nope[block:]
    d_own[0, :, LATENT:] = d_rope[block:]

    def weight(i, _):
        cols = pl.ds(pl.multiple_of(i * part, part), part)
        dw_sum[:, cols] += tn(nope, gkv[:, cols])
        return 0

    lax.fori_loop(0, pairs, weight, 0)

    @pl.when(step == pl.num_programs(0) - 1)
    def _():
        dw[...] = dw_sum[...].astype(BF).reshape(dw.shape)


def heads_grads(lo, q, g, lat, w):
    packs, _, rows, q_width = q.shape
    g_width = g.shape[3]
    block, window = 2 * rows, 4 * rows
    w_width = w.shape[1]
    pairs = q_width // (2 * QK)
    once = pl.BlockSpec((LATENT, w_width), lambda i: (0, 0))
    return pl.pallas_call(
        heads_kernel,
        grid=(packs,),
        in_specs=[
            pl.BlockSpec((1, 1, block), lambda i: (i, 0, 0)),
            pl.BlockSpec((1, 2, rows, q_width), lambda i: (i, 0, 0, 0)),
            pl.BlockSpec((1, 2, rows, g_width), lambda i: (i, 0, 0, 0)),
            pl.BlockSpec((1, 4, rows, WIDE), lambda i: (i, 0, 0, 0)),
            once,
        ],
        out_specs=[
            pl.BlockSpec((1, pairs, 2, rows, 2 * QK), lambda i: (i, 0, 0, 0, 0)),
            pl.BlockSpec((1, block, WIDE), lambda i: (i, 0, 0)),
            pl.BlockSpec((1, block, WIDE), lambda i: (i, 0, 0)),
            pl.BlockSpec((4, LATENT // 4, w_width), lambda i: (0, 0, 0)),
        ],
        out_shape=[
            jax.ShapeDtypeStruct((packs, pairs, 2, rows, 2 * QK), BF),
            jax.ShapeDtypeStruct((packs, block, WIDE), BF),
            jax.ShapeDtypeStruct((packs, block, WIDE), BF),
            jax.ShapeDtypeStruct((4, LATENT // 4, w_width), BF),
        ],
        scratch_shapes=[
            pltpu.VMEM((window, w_width), BF),
            pltpu.VMEM((window, w_width), BF),
            pltpu.VMEM((2, window, block), BF),
            pltpu.VMEM((2, window, block), BF),
            pltpu.VMEM((LATENT, w_width), F32),
            pltpu.VMEM((window, ROPE), F32),
        ],
        compiler_params=pltpu.CompilerParams(
            dimension_semantics=("arbitrary",), vmem_limit_bytes=50 * 1024 * 1024
        ),
        name="heads_grads",
    )(lo, q, g, lat, w)


def spread_kernel(gq, d_halo, d_own, dw, relay, d_lat, dw_parts, send, recv, send2, recv2):
    y, x, z, core = place()
    mine = pick(core, x, y)
    other = pick(core, y, x)
    before, after = wrap(z - 1, 8), wrap(z + 1, 8)

    for e in range(2):
        source_core = lax.rem(core + e, 2)
        axis = 1 - source_core
        spot = pick(axis, x, y)
        for d in range(4):
            if d or e:
                signal((line_dp(axis, wrap(spot - d, 4), y, x), 2 * z + source_core))
    for d in range(4):
        source = line_dp(core, wrap(mine - d, 4), y, x)
        if d:
            signal((source, 2 * z + core))
        signal((source, 2 * after + core))
    pl.semaphore_wait(pltpu.get_barrier_semaphore(), 14)

    moves = Sender()
    for d in (2, 1, 3, 0):
        there = lax.rem(other + d, 4)
        target = line_dp(1 - core, there, y, x)
        for e in range(2):
            half = lax.rem(core + e, 2)
            k = 4 * e + d
            src, dst = gq.at[:, there, half], relay.at[core, other]
            if d == 0 and e == 0:
                moves.local(src, dst, recv.at[k])
            else:
                moves.remote(src, dst, send.at[k], recv.at[k], (target, 2 * z + half))
        if d == 0:
            moves.local(dw.at[there], dw_parts.at[other], recv2.at[0, d])
        else:
            moves.remote(dw.at[there], dw_parts.at[other], send2.at[0, d], recv2.at[0, d], (target, 2 * z + core))
        there = lax.rem(mine + d, 4)
        target = line_dp(core, there, y, x)
        if d == 0:
            moves.local(d_own.at[there], d_lat.at[0, mine], recv2.at[1, d])
        else:
            moves.remote(d_own.at[there], d_lat.at[0, mine], send2.at[1, d], recv2.at[1, d], (target, 2 * z + core))
        moves.remote(d_halo.at[there], d_lat.at[1, mine], send2.at[2, d], recv2.at[2, d], (target, 2 * before + core))
    moves.finish()


def spread(gq, d_halo, d_own, dw):
    packs, pairs, _, rows, width = gq.shape
    return pl.pallas_call(
        spread_kernel,
        out_shape=[
            jax.ShapeDtypeStruct((2, 4, packs, rows, width), BF),
            jax.ShapeDtypeStruct((2, 4) + d_own.shape[1:], BF),
            jax.ShapeDtypeStruct(dw.shape, BF),
        ],
        in_specs=[ANY] * 4,
        out_specs=[ANY] * 3,
        scratch_shapes=[
            pltpu.SemaphoreType.DMA((8,)),
            pltpu.SemaphoreType.DMA((8,)),
            pltpu.SemaphoreType.DMA((3, 4)),
            pltpu.SemaphoreType.DMA((3, 4)),
        ],
        compiler_params=pltpu.CompilerParams(collective_id=1, has_side_effects=True),
        name="spread_results",
    )(gq, d_halo, d_own, dw)


def deliver_kernel(chosen, d_lat, dw, gq, lat_relay, dw_parts, send, recv, send2, recv2, send3, recv3):
    y, x, z, core = place()
    dp = 4 * y + x
    ctx = 2 * z + core
    for d in range(16):
        there = lax.rem(dp + d, 16)
        if d:
            signal((there, ctx))
        signal((there, 2 * z + 1 - core))
    for d in range(1, 8):
        signal((dp, 2 * lax.rem(z + d, 8) + core))
    pl.semaphore_wait(pltpu.get_barrier_semaphore(), 38)

    moves = Sender()
    width = chosen.shape[3]
    for d in range(16):
        there = lax.rem(dp + d, 16)
        for e in range(2):
            half = lax.rem(core + e, 2)
            src, dst = d_lat.at[half, there], lat_relay.at[dp, core]
            if d == 0 and e == 0:
                moves.local(src, dst, recv2.at[e, d])
            else:
                moves.remote(src, dst, send2.at[e, d], recv2.at[e, d], (there, 2 * z + half))
    for d in range(16):
        there = lax.rem(dp + d, 16)
        for j, at in ((0, 4 * x + y), (1, 16 + 4 * y + x)):
            dst = gq.at[:, pl.ds(pl.multiple_of(at * width, width), width)]
            if d == 0:
                moves.local(chosen.at[there, j], dst, recv.at[j, d])
            else:
                moves.remote(chosen.at[there, j], dst, send.at[j, d], recv.at[j, d], (there, ctx))
    for d in range(8):
        there = lax.rem(z + d, 8)
        if d == 0:
            moves.local(dw.at[there], dw_parts.at[z], recv3.at[d])
        else:
            moves.remote(dw.at[there], dw_parts.at[z], send3.at[d], recv3.at[d], (dp, 2 * there + core))
    moves.finish()


def deliver(chosen, d_lat, dw):
    _, _, rows, width = chosen.shape
    return pl.pallas_call(
        deliver_kernel,
        out_shape=[
            jax.ShapeDtypeStruct((rows, 32 * width), BF),
            jax.ShapeDtypeStruct((16, 2) + d_lat.shape[2:], F32),
            jax.ShapeDtypeStruct(dw.shape, F32),
        ],
        in_specs=[ANY] * 3,
        out_specs=[ANY] * 3,
        scratch_shapes=[
            pltpu.SemaphoreType.DMA((2, 16)),
            pltpu.SemaphoreType.DMA((2, 16)),
            pltpu.SemaphoreType.DMA((2, 16)),
            pltpu.SemaphoreType.DMA((2, 16)),
            pltpu.SemaphoreType.DMA((8,)),
            pltpu.SemaphoreType.DMA((8,)),
        ],
        compiler_params=pltpu.CompilerParams(collective_id=2, has_side_effects=True),
        name="deliver_queries",
    )(chosen, d_lat, dw)


def weight_home(k):
    pairs = []
    for dp in range(16):
        for ctx in range(16):
            y, x, z, core = dp // 4, dp % 4, ctx // 2, ctx % 2
            mine, other = (x, y) if core == 0 else (y, x)
            piece = k ^ (z % 2)
            home = (4 * other + z // 2) * 16 + 8 * core + 2 * mine + piece
            pairs.append((dp * 16 + ctx, home))
    return pairs


def body(queries, latent, w_kv, grad_out, doc_lengths, matching):
    y, x, z, core = place()
    dp = 4 * y + x
    rows = queries.shape[0]
    block = 2 * rows

    packs = pick(core, 4 * y + jnp.arange(4), 4 * jnp.arange(4) + x)
    ends = jnp.cumsum(doc_lengths[packs], axis=1)
    token = z * block + jnp.arange(block, dtype=jnp.int32)
    begun = jnp.where(ends[:, None, :] <= token[None, :, None], ends[:, None, :], 0)
    lo = (jnp.max(begun, axis=2) - (z - 1) * block)[:, None, :].astype(jnp.int32)

    q_all, g_all, lat_all, w_all = gather(queries, latent, w_kv, grad_out)
    w_all = w_all.reshape(LATENT, w_all.shape[2])
    gq, d_halo, d_own, dw = heads_grads(lo, q_all, g_all, lat_all, w_all)
    relay, d_lat, dw_parts = spread(gq, d_halo, d_own, dw)

    major, minor = matching // 4, lax.rem(matching, 4)
    chosen = jnp.stack([relay[0][major, minor], relay[1][minor, major]], axis=1)
    d_lat = jnp.sum(d_lat.astype(F32), axis=(0, 1)).reshape(2, 16, rows // 16, WIDE)
    dw_mine = jnp.sum(dw_parts.astype(F32), axis=0)
    dw_mine = dw_mine.reshape(8, LATENT // 32, dw_mine.shape[1])
    grad_queries, lat_relay, dw_z = deliver(chosen, d_lat, dw_mine)

    lat_chosen = jnp.sum(lat_relay, axis=1)[matching]
    grad_latent = lax.all_to_all(lat_chosen, "dp", split_axis=0, concat_axis=0, tiled=True).reshape(rows, WIDE)

    dw_last = jnp.sum(dw_z, axis=0).reshape(LATENT // 32, 2, -1)
    odd = lax.rem(z, 2)
    arrived = [
        lax.ppermute(jnp.where(odd == k, dw_last[:, 0], dw_last[:, 1]), ("dp", "ctx"), weight_home(k))
        for k in range(2)
    ]
    grad_weight = jnp.concatenate(
        [jnp.where(core == 0, arrived[0], arrived[1]), jnp.where(core == 0, arrived[1], arrived[0])], axis=0
    )
    return grad_queries, grad_latent, grad_weight


def solution(mesh):
    in_specs = (
        P(("dp", "ctx"), None),
        P(("dp", "ctx"), None),
        P(None, "ctx"),
        P(("dp", "ctx"), None),
        P(),
        P(),
    )
    out_specs = (P(("dp", "ctx"), None), P(("dp", "ctx"), None), P("dp", "ctx"))
    return jax.shard_map(body, mesh=mesh, in_specs=in_specs, out_specs=out_specs, check_vma=False)
```

```python
import functools

import jax
import jax.numpy as jnp
from jax import lax
from jax.experimental import pallas as pl
from jax.experimental.pallas import tpu as pltpu
from jax.sharding import PartitionSpec as P

NOPE = 128
ROPE = 64
VDIM = 128
LATENT = 512
HEADS = 64
ROWS = 128
QK = NOPE + ROPE
KV = NOPE + VDIM
WIDE = LATENT + ROPE
MESH = pl.DeviceIdType.MESH
ANY = pl.BlockSpec(memory_space=pl.ANY)
BF = jnp.bfloat16
F32 = jnp.float32
LOW = -1e30


def place():
    dp, ctx = lax.axis_index("dp"), lax.axis_index("ctx")
    return dp // 4, lax.rem(dp, 4), ctx // 2, lax.rem(ctx, 2)


def pick(axis, on_x, on_y):
    return (1 - axis) * on_x + axis * on_y


def wrap(value, n):
    return lax.rem(value + n, n)


def line_dp(axis, position, y, x):
    return pick(axis, 4 * y + position, 4 * position + x)


class Sender:
    def __init__(self):
        self.sent = []
        self.due = []

    def remote(self, src, dst, send_sem, recv_sem, device):
        copy = pltpu.make_async_remote_copy(
            src_ref=src, dst_ref=dst, send_sem=send_sem, recv_sem=recv_sem,
            device_id=device, device_id_type=MESH,
        )
        copy.start()
        self.sent.append(copy)
        return copy

    def local(self, src, dst, sem):
        copy = pltpu.make_async_copy(src, dst, sem)
        copy.start()
        self.due.append(copy)

    def finish(self):
        for copy in self.due:
            copy.wait()
        for copy in self.sent:
            copy.wait_recv()
        for copy in self.sent:
            copy.wait_send()


def signal(device):
    pl.semaphore_signal(pltpu.get_barrier_semaphore(), inc=1, device_id=device, device_id_type=MESH)


def block_at(position, z):
    return lax.rem(position + 8 - z, 4)


def landed(ref, sem):
    pltpu.make_async_copy(ref, ref, sem).wait()


def nt(a, b):
    return lax.dot_general(a, b, (((1,), (1,)), ((), ())), preferred_element_type=F32)


def tn(a, b):
    return lax.dot_general(a, b, (((0,), (0,)), ((), ())), preferred_element_type=F32)


def nn(a, b):
    return jnp.dot(a, b, preferred_element_type=F32)


def heads(t, lo, q, g, lat, w, gq, d_halo, d_own, kv, gkv, p_t, ds_t, dw_sum, rope_sum):
    rows = q.shape[2]
    block = 2 * rows
    window = 4 * rows
    scale = float(QK) ** -0.5
    pairs = gq.shape[1]
    part = 2 * KV
    quarter = LATENT // 4

    rope_sum[...] = jnp.zeros_like(rope_sum)
    nope = lat[t, :, :, :LATENT].reshape(window, LATENT)
    rope = lat[t, :, :, LATENT:].reshape(window, ROPE)
    lows = lo[t]
    key_at = lax.broadcasted_iota(jnp.int32, (3 * rows, rows), 0)
    query_at = lax.broadcasted_iota(jnp.int32, (3 * rows, rows), 1)

    def project(i, _):
        cols = pl.ds(pl.multiple_of(i * part, part), part)
        kv[:, cols] = nn(nope, w[:, :, cols].reshape(4 * quarter, part)).astype(BF)
        return 0

    lax.fori_loop(0, pairs, project, 0)

    def pair(i, _):
        q_two = q[t, :, :, pl.ds(pl.multiple_of(i * 2 * QK, 2 * QK), 2 * QK)].reshape(block, 2 * QK)
        g_two = g[t, :, :, pl.ds(pl.multiple_of(i * 2 * VDIM, 2 * VDIM), 2 * VDIM)].reshape(block, 2 * VDIM)
        cols = pl.ds(pl.multiple_of(i * part, part), part)
        kv_two = kv[:, cols]
        dq_two, dkv_two = [], []
        for h in range(2):
            qh = q_two[:, h * QK:(h + 1) * QK]
            gh = g_two[:, h * VDIM:(h + 1) * VDIM]
            kh = jnp.concatenate([kv_two[:, h * KV:h * KV + NOPE], rope], axis=1)
            vh = kv_two[:, h * KV + NOPE:(h + 1) * KV]
            scores = nt(kh, qh)
            dprobs = nt(vh, gh)
            for s in range(2):
                keys = slice(rows * s, rows * s + 3 * rows)
                queries = slice(rows * s, rows * s + rows)
                low = lows[:, queries] - rows * s
                seen = (key_at >= low) & (key_at <= query_at + block)
                sc = jnp.where(seen, scores[keys, queries] * scale, LOW)
                top = jnp.max(sc, axis=0, keepdims=True)
                ex = jnp.exp(sc - top)
                probs = ex * (1.0 / jnp.sum(ex, axis=0, keepdims=True))
                probs_low = probs.astype(BF)
                dp = dprobs[keys, queries]
                row_dot = jnp.sum(probs_low.astype(F32) * dp, axis=0, keepdims=True)
                p_t[h, keys, queries] = probs_low
                ds_t[h, keys, queries] = (probs * (dp - row_dot)).astype(BF)
            ds = ds_t[h]
            dq_two.append((tn(ds, kh) * scale).astype(BF))
            dk = nn(ds, qh) * scale
            dv = nn(p_t[h], gh)
            rope_sum[...] += dk[:, NOPE:]
            dkv_two += [dk[:, :NOPE].astype(BF), dv.astype(BF)]
        gkv[:, cols] = jnp.concatenate(dkv_two, axis=1)
        gq[t, i] = jnp.concatenate(dq_two, axis=1).reshape(2, rows, 2 * QK)
        return 0

    lax.fori_loop(0, pairs, pair, 0)

    d_nope = nt(gkv[...], w[...].reshape(4 * quarter, -1)).astype(BF)
    d_rope = rope_sum[...].astype(BF)
    d_halo[t, :, :LATENT] = d_nope[:block]
    d_halo[t, :, LATENT:] = d_rope[:block]
    d_own[t, :, :LATENT] = d_nope[block:]
    d_own[t, :, LATENT:] = d_rope[block:]

    def weight(i, _):
        cols = pl.ds(pl.multiple_of(i * part, part), part)
        dw_sum[:, cols] += tn(nope, gkv[:, cols])
        return 0

    lax.fori_loop(0, pairs, weight, 0)


def main_kernel(
    lo, q, latent, w, g,
    relay, d_latent, d_weight,
    q_all, g_all, lat_all, w_all, gq, d_halo, d_own, dw, d_lat, dw_parts,
    kv, gkv, p_t, ds_t, dw_sum, rope_sum,
    send, recv, w_send, w_recv, w_send2, w_recv2, gq_send, gq_recv, d_send, d_recv, dw_send, dw_recv,
):
    y, x, z, core = place()
    dp = 4 * y + x
    mine = pick(core, x, y)
    other = pick(core, y, x)
    before, after = wrap(z - 1, 8), wrap(z + 1, 8)

    w_axis = lax.rem(z, 2)
    w_first = lax.rem(pick(w_axis, x, y) + 4 - z // 2, 4)
    w_other = pick(w_axis, y, x)
    w_plane = 2 * block_at(mine, z) + core

    for e in range(2):
        half = lax.rem(core + e, 2)
        for d in range(4):
            source = line_dp(core, wrap(mine - d, 4), y, x)
            if d or e:
                signal((source, 2 * z + half))
            signal((source, 2 * before + half))
            axis = 1 - half
            source = line_dp(axis, wrap(pick(axis, x, y) - d, 4), y, x)
            if d or e:
                signal((source, 2 * z + half))
    for d in range(4):
        signal((line_dp(core, wrap(mine - d, 4), y, x), 2 * after + core))
    for b in range(2):
        @pl.when((w_plane != z) | (core != b))
        def _():
            signal((dp, 2 * w_plane + b))

    own_w = jnp.where((w_axis == core) & (lax.rem(z, 4) == w_first), 1, 0)
    pl.semaphore_wait(pltpu.get_barrier_semaphore(), 7 + 8 + 7 + 4 + 2 - own_w)

    moves = Sender()
    quarter = LATENT // 4
    w_width = w.shape[1]
    w_rows = w.at[pl.ds(pl.multiple_of(w_other * quarter, quarter), quarter)]

    def w_slot(part, b):
        return w_all.at[part, :, pl.ds(pl.multiple_of(b * w_width, w_width), w_width)]

    def w_here(i):
        return (w_axis == core) & (w_first + 4 * i == z)

    def w_copy(i):
        return pltpu.make_async_remote_copy(
            src_ref=w_rows, dst_ref=w_slot(w_other, core), send_sem=w_send.at[i], recv_sem=w_recv.at[core],
            device_id=(dp, 2 * (w_first + 4 * i) + w_axis), device_id_type=MESH,
        )

    for i in range(2):
        @pl.when(w_here(i))
        def _():
            pltpu.make_async_copy(w_rows, w_slot(w_other, core), w_recv.at[core]).start()

        @pl.when(jnp.logical_not(w_here(i)))
        def _():
            w_copy(i).start()

    q_width = q.shape[1] // 8
    g_width = g.shape[1] // 8

    def send_rows(d, e):
        axis = lax.rem(core + e, 2)
        spot = pick(axis, x, y)
        there = lax.rem(spot + d, 4)
        target = (line_dp(axis, there, y, x), 2 * z + axis)
        k = 4 * e + d
        at = 2 * block_at(there, z) + axis
        q_part = q.at[:, pl.ds(pl.multiple_of(at * q_width, q_width), q_width)]
        g_part = g.at[:, pl.ds(pl.multiple_of(at * g_width, g_width), g_width)]
        lat_own = lat_all.at[spot, 2 + core]
        if d == 0 and e == 0:
            moves.local(latent, lat_own, recv.at[2, k])
            moves.local(q_part, q_all.at[spot, core], recv.at[0, k])
            moves.local(g_part, g_all.at[spot, core], recv.at[1, k])
        else:
            moves.remote(latent, lat_own, send.at[2, k], recv.at[2, k], target)
            moves.remote(q_part, q_all.at[spot, core], send.at[0, k], recv.at[0, k], target)
            moves.remote(g_part, g_all.at[spot, core], send.at[1, k], recv.at[1, k], target)
        target = (line_dp(axis, there, y, x), 2 * after + axis)
        moves.remote(latent, lat_all.at[spot, core], send.at[3, k], recv.at[3, k], target)

    for d in range(2):
        for e in range(2):
            send_rows(d, e)
    for b in range(2):
        landed(w_slot(other, b), w_recv.at[b])
    for d in range(1, 4):
        target = (line_dp(1 - core, lax.rem(other + d, 4), y, x), 2 * z + core)
        moves.remote(w_all.at[other], w_all.at[other], w_send2.at[d], w_recv2.at[d], target)
    for d in (3, 2):
        for e in range(2):
            send_rows(d, e)
    p_t[...] = jnp.zeros_like(p_t)
    ds_t[...] = jnp.zeros_like(ds_t)
    dw_sum[...] = jnp.zeros_like(dw_sum)
    for d in range(1, 4):
        landed(w_all.at[wrap(other - d, 4)], w_recv2.at[d])

    def gq_copy(s, there, slot, e, d, half):
        return pltpu.make_async_remote_copy(
            src_ref=gq.at[slot, there, half], dst_ref=relay.at[core, other, slot],
            send_sem=gq_send.at[4 * e + d, s], recv_sem=gq_recv.at[4 * e + d, s],
            device_id=(line_dp(1 - core, there, y, x), 2 * z + half), device_id_type=MESH,
        )

    def d_copy(s, slot, kind):
        target = (line_dp(core, slot, y, x), 2 * (z if kind == 0 else before) + core)
        return pltpu.make_async_remote_copy(
            src_ref=(d_own, d_halo)[kind].at[slot], dst_ref=d_lat.at[kind, mine],
            send_sem=d_send.at[kind, s], recv_sem=d_recv.at[kind, s],
            device_id=target, device_id_type=MESH,
        )

    def order(s):
        return s + (s // 2) * (1 - 2 * lax.rem(s, 2))

    def step(s, _):
        d = order(s)
        slot = lax.rem(mine + 4 - d, 4)
        for e in range(2):
            k = 4 * e + d
            half = lax.rem(core + e, 2)
            landed(q_all.at[slot, half], recv.at[0, k])
            landed(g_all.at[slot, half], recv.at[1, k])
            landed(lat_all.at[slot, 2 + half], recv.at[2, k])
            landed(lat_all.at[slot, half], recv.at[3, k])
        heads(slot, lo, q_all, g_all, lat_all, w_all, gq, d_halo, d_own, kv, gkv, p_t, ds_t, dw_sum, rope_sum)
        for dm in (2, 1, 3, 0):
            there = lax.rem(other + dm, 4)
            for e in range(2):
                half = lax.rem(core + e, 2)
                if dm == 0 and e == 0:
                    pltpu.make_async_copy(
                        gq.at[slot, there, half], relay.at[core, other, slot], gq_recv.at[0, s]
                    ).start()
                else:
                    gq_copy(s, there, slot, e, dm, half).start()
        d_copy(s, slot, 1).start()

        @pl.when(s == 0)
        def _():
            pltpu.make_async_copy(d_own.at[slot], d_lat.at[0, mine], d_recv.at[0, s]).start()

        @pl.when(s > 0)
        def _():
            d_copy(s, slot, 0).start()

        return 0

    lax.fori_loop(0, 4, step, 0)

    dw[...] = dw_sum[...].astype(BF).reshape(dw.shape)
    for d in (2, 1, 3, 0):
        there = lax.rem(other + d, 4)
        if d == 0:
            late = pltpu.make_async_copy(dw.at[there], dw_parts.at[other], dw_recv.at[d])
            late.start()
        else:
            target = (line_dp(1 - core, there, y, x), 2 * z + core)
            late = pltpu.make_async_remote_copy(
                src_ref=dw.at[there], dst_ref=dw_parts.at[other], send_sem=dw_send.at[d], recv_sem=dw_recv.at[d],
                device_id=target, device_id_type=MESH,
            )
            late.start()

    def collect(s, _):
        d = order(s)
        landed(d_lat.at[0, lax.rem(mine + d, 4)], d_recv.at[0, s])
        landed(d_lat.at[1, lax.rem(mine + d, 4)], d_recv.at[1, s])
        return 0

    lax.fori_loop(0, 4, collect, 0)
    total = jnp.zeros(d_latent.shape, F32)
    for kind in range(2):
        for i in range(4):
            total += d_lat[kind, i].astype(F32)
    d_latent[...] = total
    for d in range(4):
        landed(dw_parts.at[lax.rem(other + 4 - d, 4)], dw_recv.at[d])
    total = jnp.zeros(d_weight.shape, F32)
    for i in range(4):
        total += dw_parts[i].astype(F32)
    d_weight[...] = total

    for copy in moves.sent:
        copy.wait_send()
    for i in range(2):
        @pl.when(jnp.logical_not(w_here(i)))
        def _():
            w_copy(i).wait_send()
    for d in range(1, 4):
        landed(dw.at[lax.rem(other + d, 4)], dw_send.at[d])

    def close(s, _):
        d = order(s)
        slot = lax.rem(mine + 4 - d, 4)
        for dm in range(4):
            for e in range(2):
                landed(relay.at[core, other, slot], gq_recv.at[4 * e + dm, s])
                if dm or e:
                    landed(gq.at[slot, 0, 0], gq_send.at[4 * e + dm, s])
        landed(d_halo.at[slot], d_send.at[1, s])

        @pl.when(s > 0)
        def _():
            landed(d_own.at[slot], d_send.at[0, s])

        return 0

    lax.fori_loop(0, 4, close, 0)


def main_part(lo, q, latent, w, g):
    rows = q.shape[0]
    block, window = 2 * rows, 4 * rows
    q_width, g_width, w_width = q.shape[1] // 8, g.shape[1] // 8, 2 * w.shape[1]
    pairs = q_width // (2 * QK)
    dma = pltpu.SemaphoreType.DMA
    vmem = pl.BlockSpec(memory_space=pltpu.VMEM)
    return pl.pallas_call(
        main_kernel,
        out_shape=[
            jax.ShapeDtypeStruct((2, 4, 4, rows, 2 * QK), BF),
            jax.ShapeDtypeStruct((block, WIDE), F32),
            jax.ShapeDtypeStruct((LATENT // 4, w_width), F32),
        ],
        in_specs=[vmem] + [ANY] * 4,
        out_specs=[ANY, vmem, vmem],
        scratch_shapes=[
            pltpu.VMEM((4, 2, rows, q_width), BF),
            pltpu.VMEM((4, 2, rows, g_width), BF),
            pltpu.VMEM((4, 4, rows, WIDE), BF),
            pltpu.VMEM((4, LATENT // 4, w_width), BF),
            pltpu.VMEM((4, pairs, 2, rows, 2 * QK), BF),
            pltpu.VMEM((4, block, WIDE), BF),
            pltpu.VMEM((4, block, WIDE), BF),
            pltpu.VMEM((4, LATENT // 4, w_width), BF),
            pltpu.VMEM((2, 4, block, WIDE), BF),
            pltpu.VMEM((4, LATENT // 4, w_width), BF),
            pltpu.VMEM((window, w_width), BF),
            pltpu.VMEM((window, w_width), BF),
            pltpu.VMEM((2, window, block), BF),
            pltpu.VMEM((2, window, block), BF),
            pltpu.VMEM((LATENT, w_width), F32),
            pltpu.VMEM((window, ROPE), F32),
            dma((4, 8)), dma((4, 8)), dma((2,)), dma((2,)), dma((4,)), dma((4,)),
            dma((8, 4)), dma((8, 4)), dma((2, 4)), dma((2, 4)), dma((4,)), dma((4,)),
        ],
        compiler_params=pltpu.CompilerParams(
            collective_id=0, has_side_effects=True, vmem_limit_bytes=56 * 1024 * 1024
        ),
        name="heads_and_exchanges",
    )(lo, q, latent, w, g)


def deliver_kernel(chosen, d_lat, dw, gq, lat_relay, dw_parts, send, recv, send2, recv2, send3, recv3):
    y, x, z, core = place()
    dp = 4 * y + x
    ctx = 2 * z + core
    for d in range(16):
        there = lax.rem(dp + d, 16)
        if d:
            signal((there, ctx))
        signal((there, 2 * z + 1 - core))
    mine = pick(core, x, y)
    part = block_at(mine, z)

    def dw_home(plane):
        return line_dp(core, lax.rem(part + plane, 4), y, x), 2 * plane + core

    for d in range(1, 8):
        signal(dw_home(lax.rem(z + d, 8)))
    pl.semaphore_wait(pltpu.get_barrier_semaphore(), 38)

    moves = Sender()
    width = chosen.shape[3]
    for d in range(16):
        there = lax.rem(dp + d, 16)
        for e in range(2):
            half = lax.rem(core + e, 2)
            src, dst = d_lat.at[half, there], lat_relay.at[dp, core]
            if d == 0 and e == 0:
                moves.local(src, dst, recv2.at[e, d])
            else:
                moves.remote(src, dst, send2.at[e, d], recv2.at[e, d], (there, 2 * z + half))
    for d in range(16):
        there = lax.rem(dp + d, 16)
        for j, at in ((0, 8 * block_at(x, z) + y), (1, 8 * block_at(y, z) + 4 + x)):
            dst = gq.at[:, pl.ds(pl.multiple_of(at * width, width), width)]
            if d == 0:
                moves.local(chosen.at[there, j], dst, recv.at[j, d])
            else:
                moves.remote(chosen.at[there, j], dst, send.at[j, d], recv.at[j, d], (there, ctx))
    for d in range(8):
        there = lax.rem(z + d, 8)
        if d == 0:
            moves.local(dw.at[there], dw_parts.at[z], recv3.at[d])
        else:
            moves.remote(dw.at[there], dw_parts.at[z], send3.at[d], recv3.at[d], dw_home(there))
    moves.finish()


def deliver(chosen, d_lat, dw):
    _, _, rows, width = chosen.shape
    return pl.pallas_call(
        deliver_kernel,
        out_shape=[
            jax.ShapeDtypeStruct((rows, 32 * width), BF),
            jax.ShapeDtypeStruct((16, 2) + d_lat.shape[2:], F32),
            jax.ShapeDtypeStruct(dw.shape, F32),
        ],
        in_specs=[ANY] * 3,
        out_specs=[ANY] * 3,
        scratch_shapes=[
            pltpu.SemaphoreType.DMA((2, 16)),
            pltpu.SemaphoreType.DMA((2, 16)),
            pltpu.SemaphoreType.DMA((2, 16)),
            pltpu.SemaphoreType.DMA((2, 16)),
            pltpu.SemaphoreType.DMA((8,)),
            pltpu.SemaphoreType.DMA((8,)),
        ],
        compiler_params=pltpu.CompilerParams(collective_id=2, has_side_effects=True),
        name="deliver_queries",
    )(chosen, d_lat, dw)


def weight_home(k):
    pairs = []
    for dp in range(16):
        for ctx in range(16):
            y, x, z, core = dp // 4, dp % 4, ctx // 2, ctx % 2
            mine, other = (x, y) if core == 0 else (y, x)
            piece = k ^ (z % 2)
            home = (4 * other + z // 2) * 16 + 4 * ((mine - z) % 4) + 2 * core + piece
            pairs.append((dp * 16 + ctx, home))
    return pairs


def body(queries, latent, w_kv, grad_out, doc_lengths, matching):
    y, x, z, core = place()
    dp = 4 * y + x
    rows = queries.shape[0]
    block = 2 * rows

    packs = pick(core, 4 * y + jnp.arange(4), 4 * jnp.arange(4) + x)
    ends = jnp.cumsum(doc_lengths[packs], axis=1)
    token = z * block + jnp.arange(block, dtype=jnp.int32)
    begun = jnp.where(ends[:, None, :] <= token[None, :, None], ends[:, None, :], 0)
    lo = (jnp.max(begun, axis=2) - (z - 1) * block)[:, None, :].astype(jnp.int32)

    relay, d_lat, dw_mine = main_part(lo, queries, latent, w_kv, grad_out)

    major, minor = matching // 4, lax.rem(matching, 4)
    chosen = jnp.stack([relay[0][major, minor], relay[1][minor, major]], axis=1)
    d_lat = d_lat.reshape(2, 16, rows // 16, WIDE)
    dw_mine = dw_mine.reshape(8, LATENT // 32, dw_mine.shape[1])
    grad_queries, lat_relay, dw_z = deliver(chosen, d_lat, dw_mine)

    lat_chosen = jnp.sum(lat_relay, axis=1)[matching]
    grad_latent = lax.all_to_all(lat_chosen, "dp", split_axis=0, concat_axis=0, tiled=True).reshape(rows, WIDE)

    dw_last = jnp.sum(dw_z, axis=0).reshape(LATENT // 32, 2, -1)
    odd = lax.rem(z, 2)
    arrived = [
        lax.ppermute(jnp.where(odd == k, dw_last[:, 0], dw_last[:, 1]), ("dp", "ctx"), weight_home(k))
        for k in range(2)
    ]
    grad_weight = jnp.concatenate(
        [jnp.where(core == 0, arrived[0], arrived[1]), jnp.where(core == 0, arrived[1], arrived[0])], axis=0
    )
    return grad_queries, grad_latent, grad_weight


def solution(mesh):
    in_specs = (
        P(("dp", "ctx"), None),
        P(("dp", "ctx"), None),
        P(None, "ctx"),
        P(("dp", "ctx"), None),
        P(),
        P(),
    )
    out_specs = (P(("dp", "ctx"), None), P(("dp", "ctx"), None), P("dp", "ctx"))
    return jax.shard_map(body, mesh=mesh, in_specs=in_specs, out_specs=out_specs, check_vma=False)
```

```python
import jax
import jax.numpy as jnp
from jax import lax
from jax.experimental import pallas as pl
from jax.experimental.pallas import tpu as pltpu
from jax.sharding import PartitionSpec as P

NOPE = 128
ROPE = 64
VDIM = 128
LATENT = 512
HEADS = 64
ROWS = 128
QK = NOPE + ROPE
KV = NOPE + VDIM
WIDE = LATENT + ROPE
MESH = pl.DeviceIdType.MESH
ANY = pl.BlockSpec(memory_space=pl.ANY)
BF = jnp.bfloat16
F32 = jnp.float32
LOW = -1e30


def place():
    dp, ctx = lax.axis_index("dp"), lax.axis_index("ctx")
    return dp // 4, lax.rem(dp, 4), ctx // 2, lax.rem(ctx, 2)


def pick(axis, on_x, on_y):
    return (1 - axis) * on_x + axis * on_y


def wrap(value, n):
    return lax.rem(value + n, n)


def line_dp(axis, position, y, x):
    return pick(axis, 4 * y + position, 4 * position + x)


class Sender:
    def __init__(self):
        self.sent = []
        self.due = []

    def remote(self, src, dst, send_sem, recv_sem, device):
        copy = pltpu.make_async_remote_copy(
            src_ref=src, dst_ref=dst, send_sem=send_sem, recv_sem=recv_sem,
            device_id=device, device_id_type=MESH,
        )
        copy.start()
        self.sent.append(copy)
        return copy

    def local(self, src, dst, sem):
        copy = pltpu.make_async_copy(src, dst, sem)
        copy.start()
        self.due.append(copy)


def signal(device):
    pl.semaphore_signal(pltpu.get_barrier_semaphore(), inc=1, device_id=device, device_id_type=MESH)


def block_at(position, z):
    return lax.rem(position + 8 - z, 4)


def landed(ref, sem):
    pltpu.make_async_copy(ref, ref, sem).wait()


def nt(a, b):
    return lax.dot_general(a, b, (((1,), (1,)), ((), ())), preferred_element_type=F32)


def tn(a, b):
    return lax.dot_general(a, b, (((0,), (0,)), ((), ())), preferred_element_type=F32)


def nn(a, b):
    return jnp.dot(a, b, preferred_element_type=F32)


def heads(t, lo, q, g, lat, w, gq, d_halo, d_own, kv, gkv, p_t, ds_t, dw_sum, rope_sum):
    rows = q.shape[2]
    block = 2 * rows
    window = 4 * rows
    scale = float(QK) ** -0.5
    pairs = gq.shape[1]
    part = 2 * KV
    quarter = LATENT // 4

    rope_sum[...] = jnp.zeros_like(rope_sum)
    nope = lat[t, :, :, :LATENT].reshape(window, LATENT)
    rope = lat[t, :, :, LATENT:].reshape(window, ROPE)
    lows = lo[t]
    key_at = lax.broadcasted_iota(jnp.int32, (3 * rows, rows), 0)
    query_at = lax.broadcasted_iota(jnp.int32, (3 * rows, rows), 1)

    def project(i, _):
        cols = pl.ds(pl.multiple_of(i * part, part), part)
        kv[:, cols] = nn(nope, w[:, :, cols].reshape(4 * quarter, part)).astype(BF)
        return 0

    lax.fori_loop(0, pairs, project, 0)

    def pair(i, _):
        q_two = q[t, :, :, pl.ds(pl.multiple_of(i * 2 * QK, 2 * QK), 2 * QK)].reshape(block, 2 * QK)
        g_two = g[t, :, :, pl.ds(pl.multiple_of(i * 2 * VDIM, 2 * VDIM), 2 * VDIM)].reshape(block, 2 * VDIM)
        cols = pl.ds(pl.multiple_of(i * part, part), part)
        kv_two = kv[:, cols]
        dq_two, dkv_two = [], []
        for h in range(2):
            qh = q_two[:, h * QK:(h + 1) * QK]
            gh = g_two[:, h * VDIM:(h + 1) * VDIM]
            kh = jnp.concatenate([kv_two[:, h * KV:h * KV + NOPE], rope], axis=1)
            vh = kv_two[:, h * KV + NOPE:(h + 1) * KV]
            scores = nt(kh, qh)
            dprobs = nt(vh, gh)
            for s in range(2):
                keys = slice(rows * s, rows * s + 3 * rows)
                queries = slice(rows * s, rows * s + rows)
                low = lows[:, queries] - rows * s
                seen = (key_at >= low) & (key_at <= query_at + block)
                sc = jnp.where(seen, scores[keys, queries] * scale, LOW)
                top = jnp.max(sc, axis=0, keepdims=True)
                ex = jnp.exp(sc - top)
                probs = ex * (1.0 / jnp.sum(ex, axis=0, keepdims=True))
                probs_low = probs.astype(BF)
                dp = dprobs[keys, queries]
                row_dot = jnp.sum(probs_low.astype(F32) * dp, axis=0, keepdims=True)
                p_t[h, keys, queries] = probs_low
                ds_t[h, keys, queries] = (probs * (dp - row_dot)).astype(BF)
            ds = ds_t[h]
            dq_two.append((tn(ds, kh) * scale).astype(BF))
            dk = nn(ds, qh) * scale
            dv = nn(p_t[h], gh)
            rope_sum[...] += dk[:, NOPE:]
            dkv_two += [dk[:, :NOPE].astype(BF), dv.astype(BF)]
        gkv[:, cols] = jnp.concatenate(dkv_two, axis=1)
        gq[t, i] = jnp.concatenate(dq_two, axis=1).reshape(2, rows, 2 * QK)
        return 0

    lax.fori_loop(0, pairs, pair, 0)

    d_nope = nt(gkv[...], w[...].reshape(4 * quarter, -1))
    d_halo[t, :, :LATENT] = d_nope[:block].astype(BF)
    d_halo[t, :, LATENT:] = rope_sum[:block].astype(BF)
    d_own[t, :, :LATENT] = d_nope[block:]
    d_own[t, :, LATENT:] = rope_sum[block:]

    def weight(i, _):
        cols = pl.ds(pl.multiple_of(i * part, part), part)
        dw_sum[:, cols] += tn(nope, gkv[:, cols])
        return 0

    lax.fori_loop(0, pairs, weight, 0)


def main_kernel(
    lo, from_x, from_y, q, latent, w, g,
    grad_q, grad_lat, grad_w,
    q_all, g_all, lat_all, w_all, gq, relay, chosen, come,
    d_halo, d_in, d_own, d_line, d_lat, d_sum, d_relay, d_pick,
    dw, dw_parts, dw_total, dw_z, dw_last,
    kv, gkv, p_t, ds_t, dw_sum, rope_sum,
    send, recv, w_send, w_recv, w_send2, w_recv2, z_send, z_recv, gq_send, gq_recv, d_send, d_recv,
    a_send, a_recv, b_send, b_recv, r_send, r_recv, out_sem, dw_send, dw_recv, dz_send, dz_recv, dl_send, dl_recv,
):
    y, x, z, core = place()
    dp = 4 * y + x
    ctx = 2 * z + core
    mine = pick(core, x, y)
    other = pick(core, y, x)
    before, after = wrap(z - 1, 8), wrap(z + 1, 8)
    rows = q.shape[0]
    quarter = LATENT // 4
    w_width = w.shape[1]

    w_axis = lax.rem(z, 2)
    w_first = lax.rem(pick(w_axis, x, y) + 4 - z // 2, 4)
    w_other = pick(w_axis, y, x)
    part = block_at(mine, z)
    w_plane = 2 * part + core

    def dw_mate(plane):
        return line_dp(core, lax.rem(part + plane, 4), y, x), 2 * plane + core

    def dw_home(b):
        return 4 * other + z // 2, 2 * w_plane + b

    def dw_source(odd):
        plane = 2 * x + odd
        spot = lax.rem(z // 2 + plane, 4)
        return pick(w_axis, 4 * y + spot, 4 * spot + y), 2 * plane + w_axis

    def is_me(device):
        return (device[0] == dp) & (device[1] == ctx)

    for d in range(16):
        there = lax.rem(dp + d, 16)
        if d:
            signal((there, ctx))
        signal((there, 2 * z + 1 - core))
    signal((dp, 2 * before + core))
    signal((dp, 2 * after + core))
    for d in range(1, 8):
        signal(dw_mate(lax.rem(z + d, 8)))
    strangers = 0
    for b in range(2):
        @pl.when(jnp.logical_not(is_me((dp, 2 * w_plane + b))))
        def _():
            signal((dp, 2 * w_plane + b))

        @pl.when(jnp.logical_not(is_me(dw_source(b))))
        def _():
            signal(dw_source(b))

        strangers += jnp.where(is_me((dp, 2 * (w_first + 4 * b) + w_axis)), 0, 1)
        strangers += jnp.where(is_me(dw_home(b)), 0, 1)

    pl.semaphore_wait(pltpu.get_barrier_semaphore(), 31 + 2 + 7 + strangers)

    moves = Sender()
    w_rows = w.at[pl.ds(pl.multiple_of(w_other * quarter, quarter), quarter)]

    def w_slot(at, b):
        return w_all.at[at, :, pl.ds(pl.multiple_of(b * w_width, w_width), w_width)]

    def w_here(i):
        return is_me((dp, 2 * (w_first + 4 * i) + w_axis))

    def w_copy(i):
        return pltpu.make_async_remote_copy(
            src_ref=w_rows, dst_ref=w_slot(w_other, core), send_sem=w_send.at[i], recv_sem=w_recv.at[core],
            device_id=(dp, 2 * (w_first + 4 * i) + w_axis), device_id_type=MESH,
        )

    for i in range(2):
        @pl.when(w_here(i))
        def _():
            pltpu.make_async_copy(w_rows, w_slot(w_other, core), w_recv.at[core]).start()

        @pl.when(jnp.logical_not(w_here(i)))
        def _():
            w_copy(i).start()

    q_width = q.shape[1] // 8
    g_width = g.shape[1] // 8

    def send_latent(d, e):
        axis = lax.rem(core + e, 2)
        spot = pick(axis, x, y)
        k = 4 * e + d
        dst = lat_all.at[spot, 2 + core]
        if d == 0 and e == 0:
            moves.local(latent, dst, recv.at[2, k])
        else:
            target = (line_dp(axis, lax.rem(spot + d, 4), y, x), 2 * z + axis)
            moves.remote(latent, dst, send.at[2, k], recv.at[2, k], target)

    def send_rows(d, e):
        axis = lax.rem(core + e, 2)
        spot = pick(axis, x, y)
        there = lax.rem(spot + d, 4)
        target = (line_dp(axis, there, y, x), 2 * z + axis)
        k = 4 * e + d
        at = 2 * block_at(there, z) + axis
        q_part = q.at[:, pl.ds(pl.multiple_of(at * q_width, q_width), q_width)]
        g_part = g.at[:, pl.ds(pl.multiple_of(at * g_width, g_width), g_width)]
        if d == 0 and e == 0:
            moves.local(q_part, q_all.at[spot, core], recv.at[0, k])
            moves.local(g_part, g_all.at[spot, core], recv.at[1, k])
        else:
            moves.remote(q_part, q_all.at[spot, core], send.at[0, k], recv.at[0, k], target)
            moves.remote(g_part, g_all.at[spot, core], send.at[1, k], recv.at[1, k], target)

    def forward_latent(d):
        slot = wrap(mine - d, 4)
        for e in range(2):
            landed(lat_all.at[slot, 2 + lax.rem(core + e, 2)], recv.at[2, 4 * e + d])
        moves.remote(
            lat_all.at[slot, pl.ds(2, 2)], lat_all.at[slot, pl.ds(0, 2)],
            z_send.at[0, d], z_recv.at[0, d], (dp, 2 * after + core),
        )

    for d in range(4):
        for e in range(2):
            send_latent(d, e)
    for d in range(2):
        for e in range(2):
            send_rows(d, e)
    forward_latent(0)
    for b in range(2):
        landed(w_slot(other, b), w_recv.at[b])
    for d in range(1, 4):
        target = (line_dp(1 - core, lax.rem(other + d, 4), y, x), 2 * z + core)
        moves.remote(w_all.at[other], w_all.at[other], w_send2.at[d], w_recv2.at[d], target)
    for d in (3, 2):
        for e in range(2):
            send_rows(d, e)
    for d in (1, 3, 2):
        forward_latent(d)
    p_t[...] = jnp.zeros_like(p_t)
    ds_t[...] = jnp.zeros_like(ds_t)
    dw_sum[...] = jnp.zeros_like(dw_sum)
    for d in range(1, 4):
        landed(w_all.at[wrap(other - d, 4)], w_recv2.at[d])

    def gq_copy(s, there, slot, e, d, half):
        return pltpu.make_async_remote_copy(
            src_ref=gq.at[slot, there, half], dst_ref=relay.at[core, 4 * other + slot],
            send_sem=gq_send.at[4 * e + d, s], recv_sem=gq_recv.at[4 * e + d, s],
            device_id=(line_dp(1 - core, there, y, x), 2 * z + half), device_id_type=MESH,
        )

    def halo_copy(s, slot):
        return pltpu.make_async_remote_copy(
            src_ref=d_halo.at[slot], dst_ref=d_in.at[slot], send_sem=z_send.at[1, s], recv_sem=z_recv.at[1, s],
            device_id=(dp, 2 * before + core), device_id_type=MESH,
        )

    def d_copy(s, slot):
        return pltpu.make_async_remote_copy(
            src_ref=d_line.at[slot], dst_ref=d_lat.at[mine], send_sem=d_send.at[s], recv_sem=d_recv.at[s],
            device_id=(line_dp(core, slot, y, x), 2 * z + core), device_id_type=MESH,
        )

    def order(s):
        return s + (s // 2) * (1 - 2 * lax.rem(s, 2))

    def slot_of(s):
        return lax.rem(mine + 4 - order(s), 4)

    def add_halo(s):
        slot = slot_of(s)
        landed(d_in.at[slot], z_recv.at[1, s])
        d_line[slot] = (d_own[slot] + d_in[slot].astype(F32)).astype(BF)

        @pl.when(s == 0)
        def _():
            pltpu.make_async_copy(d_line.at[slot], d_lat.at[mine], d_recv.at[s]).start()

        @pl.when(s > 0)
        def _():
            d_copy(s, slot).start()

    def step(s, _):
        d = order(s)
        slot = slot_of(s)
        for e in range(2):
            half = lax.rem(core + e, 2)
            landed(q_all.at[slot, half], recv.at[0, 4 * e + d])
            landed(g_all.at[slot, half], recv.at[1, 4 * e + d])
        landed(lat_all.at[slot, pl.ds(0, 2)], z_recv.at[0, d])
        heads(slot, lo, q_all, g_all, lat_all, w_all, gq, d_halo, d_own, kv, gkv, p_t, ds_t, dw_sum, rope_sum)
        halo_copy(s, slot).start()
        for dm in (2, 1, 3, 0):
            there = lax.rem(other + dm, 4)
            for e in range(2):
                half = lax.rem(core + e, 2)
                if dm == 0 and e == 0:
                    pltpu.make_async_copy(
                        gq.at[slot, there, half], relay.at[core, 4 * other + slot], gq_recv.at[0, s]
                    ).start()
                else:
                    gq_copy(s, there, slot, e, dm, half).start()

        @pl.when(s > 0)
        def _():
            add_halo(s - 1)

        return 0

    lax.fori_loop(0, 4, step, 0)

    dw[...] = dw_sum[...].astype(BF).reshape(dw.shape)
    for d in (2, 1, 3, 0):
        there = lax.rem(other + d, 4)
        if d == 0:
            moves.local(dw.at[there], dw_parts.at[other], dw_recv.at[d])
        else:
            target = (line_dp(1 - core, there, y, x), 2 * z + core)
            moves.remote(dw.at[there], dw_parts.at[other], dw_send.at[d], dw_recv.at[d], target)
    add_halo(jnp.int32(3))

    def relayed(s, _):
        for k in range(8):
            landed(relay.at[core, 4 * other], gq_recv.at[k, s])
        return 0

    lax.fori_loop(0, 4, relayed, 0)

    def deliver(d):
        there = lax.rem(dp + d, 16)
        chosen[there, 0] = relay[0, from_x[there]]
        chosen[there, 1] = relay[1, from_y[there]]
        if d == 0:
            moves.local(chosen.at[there], come.at[dp], r_recv.at[d])
        else:
            moves.remote(chosen.at[there], come.at[dp], r_send.at[d], r_recv.at[d], (there, ctx))

    for d in range(15, -1, -1):
        deliver(d)

    def collect(s, _):
        landed(d_lat.at[lax.rem(mine + order(s), 4)], d_recv.at[s])
        return 0

    lax.fori_loop(0, 4, collect, 0)
    total = d_lat[0].astype(F32)
    for i in range(1, 4):
        total += d_lat[i].astype(F32)
    d_sum[...] = total.reshape(d_sum.shape)
    for d in range(16):
        there = lax.rem(dp + d, 16)
        for e in range(2):
            half = lax.rem(core + e, 2)
            if d == 0 and e == 0:
                moves.local(d_sum.at[half, there], d_relay.at[dp, core], a_recv.at[e, d])
            else:
                moves.remote(
                    d_sum.at[half, there], d_relay.at[dp, core], a_send.at[e, d], a_recv.at[e, d],
                    (there, 2 * z + half),
                )

    for d in range(4):
        landed(dw_parts.at[wrap(other - d, 4)], dw_recv.at[d])
    total = dw_parts[0].astype(F32)
    for i in range(1, 4):
        total += dw_parts[i].astype(F32)
    dw_total[...] = total.reshape(dw_total.shape)
    for d in range(8):
        there = lax.rem(z + d, 8)
        if d == 0:
            moves.local(dw_total.at[there], dw_z.at[z], dz_recv.at[d])
        else:
            moves.remote(dw_total.at[there], dw_z.at[z], dz_send.at[d], dz_recv.at[d], dw_mate(there))

    for d in range(16):
        for e in range(2):
            landed(d_relay.at[dp, core], a_recv.at[e, d])
    for d in range(16):
        there = lax.rem(dp + d, 16)
        d_pick[there] = d_relay[from_x[there], 0] + d_relay[from_x[there], 1]
        if d == 0:
            moves.local(d_pick.at[there], grad_lat.at[dp], b_recv.at[d])
        else:
            moves.remote(d_pick.at[there], grad_lat.at[dp], b_send.at[d], b_recv.at[d], (there, ctx))

    for d in range(8):
        landed(dw_z.at[wrap(z - d, 8)], dz_recv.at[d])
    total = dw_z[0]
    for i in range(1, 8):
        total += dw_z[i]
    for b in range(2):
        dw_last[b] = total[:, b * w_width:(b + 1) * w_width]
    odd = lax.rem(z, 2)

    def last_copy(b):
        return pltpu.make_async_remote_copy(
            src_ref=dw_last.at[b], dst_ref=grad_w.at[odd], send_sem=dl_send.at[b], recv_sem=dl_recv.at[odd],
            device_id=dw_home(b), device_id_type=MESH,
        )

    for b in range(2):
        @pl.when(is_me(dw_home(b)))
        def _():
            pltpu.make_async_copy(dw_last.at[b], grad_w.at[odd], dl_recv.at[odd]).start()

        @pl.when(jnp.logical_not(is_me(dw_home(b))))
        def _():
            last_copy(b).start()

    width = relay.shape[3]
    parts = []
    for d in range(15, -1, -1):
        source = wrap(dp - d, 16)
        landed(come.at[source], r_recv.at[d])
        sy, sx = source // 4, lax.rem(source, 4)
        for j, at in ((0, 8 * block_at(sx, z) + sy), (1, 8 * block_at(sy, z) + 4 + sx)):
            dst = grad_q.at[:, pl.ds(pl.multiple_of(at * width, width), width)]
            copy = pltpu.make_async_copy(come.at[source, j], dst, out_sem.at[d, j])
            copy.start()
            parts.append(copy)

    for d in range(16):
        landed(d_pick.at[dp], b_recv.at[d])
    for b in range(2):
        landed(dw_last.at[b], dl_recv.at[b])

        @pl.when(jnp.logical_not(is_me(dw_home(b))))
        def _():
            last_copy(b).wait_send()

        @pl.when(jnp.logical_not(w_here(b)))
        def _():
            w_copy(b).wait_send()

    for copy in moves.sent:
        copy.wait_send()

    def close(s, _):
        slot = slot_of(s)
        for k in range(1, 8):
            landed(gq.at[slot, 0, 0], gq_send.at[k, s])
        landed(d_halo.at[slot], z_send.at[1, s])

        @pl.when(s > 0)
        def _():
            landed(d_line.at[slot], d_send.at[s])

        return 0

    lax.fori_loop(0, 4, close, 0)
    for copy in parts:
        copy.wait()


def main_part(lo, from_x, from_y, q, latent, w, g):
    rows = q.shape[0]
    block, window = 2 * rows, 4 * rows
    q_width, g_width, w_width = q.shape[1] // 8, g.shape[1] // 8, 2 * w.shape[1]
    pairs = q_width // (2 * QK)
    quarter = LATENT // 4
    dma = pltpu.SemaphoreType.DMA
    vmem = pl.BlockSpec(memory_space=pltpu.VMEM)
    smem = pl.BlockSpec(memory_space=pltpu.SMEM)
    return pl.pallas_call(
        main_kernel,
        out_shape=[
            jax.ShapeDtypeStruct(q.shape, BF),
            jax.ShapeDtypeStruct((16, rows // 16, WIDE), F32),
            jax.ShapeDtypeStruct((2, LATENT // 32, w.shape[1]), F32),
        ],
        in_specs=[vmem, smem, smem] + [ANY] * 4,
        out_specs=[ANY] * 3,
        scratch_shapes=[
            pltpu.VMEM((4, 2, rows, q_width), BF),
            pltpu.VMEM((4, 2, rows, g_width), BF),
            pltpu.VMEM((4, 4, rows, WIDE), BF),
            pltpu.VMEM((4, quarter, w_width), BF),
            pltpu.VMEM((4, pairs, 2, rows, 2 * QK), BF),
            pltpu.VMEM((2, 16, rows, 2 * QK), BF),
            pltpu.VMEM((16, 2, rows, 2 * QK), BF),
            pltpu.VMEM((16, 2, rows, 2 * QK), BF),
            pltpu.VMEM((4, block, WIDE), BF),
            pltpu.VMEM((4, block, WIDE), BF),
            pltpu.VMEM((4, block, WIDE), F32),
            pltpu.VMEM((4, block, WIDE), BF),
            pltpu.VMEM((4, block, WIDE), BF),
            pltpu.VMEM((2, 16, rows // 16, WIDE), F32),
            pltpu.VMEM((16, 2, rows // 16, WIDE), F32),
            pltpu.VMEM((16, rows // 16, WIDE), F32),
            pltpu.VMEM((4, quarter, w_width), BF),
            pltpu.VMEM((4, quarter, w_width), BF),
            pltpu.VMEM((8, LATENT // 32, w_width), F32),
            pltpu.VMEM((8, LATENT // 32, w_width), F32),
            pltpu.VMEM((2, LATENT // 32, w.shape[1]), F32),
            pltpu.VMEM((window, w_width), BF),
            pltpu.VMEM((window, w_width), BF),
            pltpu.VMEM((2, window, block), BF),
            pltpu.VMEM((2, window, block), BF),
            pltpu.VMEM((LATENT, w_width), F32),
            pltpu.VMEM((window, ROPE), F32),
            dma((3, 8)), dma((3, 8)), dma((2,)), dma((2,)), dma((4,)), dma((4,)), dma((2, 4)), dma((2, 4)),
            dma((8, 4)), dma((8, 4)), dma((4,)), dma((4,)),
            dma((2, 16)), dma((2, 16)), dma((16,)), dma((16,)), dma((16,)), dma((16,)), dma((16, 2)),
            dma((4,)), dma((4,)), dma((8,)), dma((8,)), dma((2,)), dma((2,)),
        ],
        compiler_params=pltpu.CompilerParams(
            collective_id=0, has_side_effects=True, vmem_limit_bytes=60 * 1024 * 1024
        ),
        name="heads_and_exchanges",
    )(lo, from_x, from_y, q, latent, w, g)


def body(queries, latent, w_kv, grad_out, doc_lengths, matching):
    y, x, z, core = place()
    dp = 4 * y + x
    rows = queries.shape[0]
    block = 2 * rows

    packs = pick(core, 4 * y + jnp.arange(4), 4 * jnp.arange(4) + x)
    ends = jnp.cumsum(doc_lengths[packs], axis=1)
    token = z * block + jnp.arange(block, dtype=jnp.int32)
    begun = jnp.where(ends[:, None, :] <= token[None, :, None], ends[:, None, :], 0)
    lo = (jnp.max(begun, axis=2) - (z - 1) * block)[:, None, :].astype(jnp.int32)

    turned = 4 * lax.rem(matching, 4) + matching // 4
    grad_queries, grad_latent, grad_weight = main_part(lo, matching, turned, queries, latent, w_kv, grad_out)
    return grad_queries, grad_latent.reshape(rows, WIDE), grad_weight.reshape(LATENT // 16, -1)


def solution(mesh):
    in_specs = (
        P(("dp", "ctx"), None),
        P(("dp", "ctx"), None),
        P(None, "ctx"),
        P(("dp", "ctx"), None),
        P(),
        P(),
    )
    out_specs = (P(("dp", "ctx"), None), P(("dp", "ctx"), None), P("dp", "ctx"))
    return jax.shard_map(body, mesh=mesh, in_specs=in_specs, out_specs=out_specs, check_vma=False)
```

```python
import jax
import jax.numpy as jnp
from jax import lax
from jax.experimental import pallas as pl
from jax.experimental.pallas import tpu as pltpu
from jax.sharding import PartitionSpec as P

NOPE = 128
ROPE = 64
VDIM = 128
LATENT = 512
HEADS = 64
ROWS = 128
QK = NOPE + ROPE
KV = NOPE + VDIM
WIDE = LATENT + ROPE
MESH = pl.DeviceIdType.MESH
ANY = pl.BlockSpec(memory_space=pl.ANY)
BF = jnp.bfloat16
F32 = jnp.float32
LOW = -1e30


def place():
    dp, ctx = lax.axis_index("dp"), lax.axis_index("ctx")
    return dp // 4, lax.rem(dp, 4), ctx // 2, lax.rem(ctx, 2)


def pick(axis, on_x, on_y):
    return (1 - axis) * on_x + axis * on_y


def wrap(value, n):
    return lax.rem(value + n, n)


def line_dp(axis, position, y, x):
    return pick(axis, 4 * y + position, 4 * position + x)


class Sender:
    def __init__(self):
        self.sent = []
        self.due = []

    def remote(self, src, dst, send_sem, recv_sem, device):
        copy = pltpu.make_async_remote_copy(
            src_ref=src, dst_ref=dst, send_sem=send_sem, recv_sem=recv_sem,
            device_id=device, device_id_type=MESH,
        )
        copy.start()
        self.sent.append(copy)
        return copy

    def local(self, src, dst, sem):
        copy = pltpu.make_async_copy(src, dst, sem)
        copy.start()
        self.due.append(copy)


def signal(device):
    pl.semaphore_signal(pltpu.get_barrier_semaphore(), inc=1, device_id=device, device_id_type=MESH)


def block_at(position, z):
    return lax.rem(position + 8 - z, 4)


def landed(ref, sem):
    pltpu.make_async_copy(ref, ref, sem).wait()


def nt(a, b):
    return lax.dot_general(a, b, (((1,), (1,)), ((), ())), preferred_element_type=F32)


def tn(a, b):
    return lax.dot_general(a, b, (((0,), (0,)), ((), ())), preferred_element_type=F32)


def nn(a, b):
    return jnp.dot(a, b, preferred_element_type=F32)


def heads(t, pair, lo, q, g, lat, w, gq, d_acc, dw_acc, p_t, ds_t):
    rows = q.shape[3]
    block = 2 * rows
    window = 4 * rows
    scale = float(QK) ** -0.5

    nope = lat[t, :, :, :LATENT].reshape(window, LATENT)
    rope = lat[t, :, :, LATENT:].reshape(window, ROPE)
    w_two = w[pair].reshape(LATENT, 2 * KV)
    lows = lo[t]
    key_at = lax.broadcasted_iota(jnp.int32, (3 * rows, rows), 0)
    query_at = lax.broadcasted_iota(jnp.int32, (3 * rows, rows), 1)
    kv_two = nn(nope, w_two).astype(BF)
    q_two = q[pair, t].reshape(block, 2 * QK)
    g_two = g[pair, t].reshape(block, 2 * VDIM)
    dq_two, dkv_two = [], []
    d_rope = None
    for h in range(2):
        qh = q_two[:, h * QK:(h + 1) * QK]
        gh = g_two[:, h * VDIM:(h + 1) * VDIM]
        kh = jnp.concatenate([kv_two[:, h * KV:h * KV + NOPE], rope], axis=1)
        vh = kv_two[:, h * KV + NOPE:(h + 1) * KV]
        scores = nt(kh, qh)
        dprobs = nt(vh, gh)
        for s in range(2):
            keys = slice(rows * s, rows * s + 3 * rows)
            queries = slice(rows * s, rows * s + rows)
            low = lows[:, queries] - rows * s
            seen = (key_at >= low) & (key_at <= query_at + block)
            sc = jnp.where(seen, scores[keys, queries] * scale, LOW)
            top = jnp.max(sc, axis=0, keepdims=True)
            ex = jnp.exp(sc - top)
            probs = ex * (1.0 / jnp.sum(ex, axis=0, keepdims=True))
            probs_low = probs.astype(BF)
            dp = dprobs[keys, queries]
            row_dot = jnp.sum(probs_low.astype(F32) * dp, axis=0, keepdims=True)
            p_t[h, keys, queries] = probs_low
            ds_t[h, keys, queries] = (probs * (dp - row_dot)).astype(BF)
        ds = ds_t[h]
        dq_two.append((tn(ds, kh) * scale).astype(BF))
        dk = nn(ds, qh) * scale
        dv = nn(p_t[h], gh)
        d_rope = dk[:, NOPE:] if d_rope is None else d_rope + dk[:, NOPE:]
        dkv_two += [dk[:, :NOPE].astype(BF), dv.astype(BF)]
    gkv = jnp.concatenate(dkv_two, axis=1)
    gq[pair, t] = jnp.concatenate(dq_two, axis=1).reshape(2, rows, 2 * QK)
    d_acc[t, :, :LATENT] += nt(gkv, w_two)
    d_acc[t, :, LATENT:] += d_rope
    dw_acc[...] += tn(nope, gkv)


def main_kernel(
    lo, from_x, from_y, q, latent, w, g,
    grad_q, grad_lat, grad_w,
    q_all, g_all, lat_all, w_all, gq, relay, relay_now, chosen, come,
    d_acc, d_halo, d_in, d_line, d_lat, d_sum, d_cross, d_relay, d_pick,
    dw, dw_parts, dw_total, dw_z, dw_last, dw_acc, p_t, ds_t,
    send, recv, l_send, l_recv, w_send, w_recv, w_send2, w_recv2, z_send, z_recv, gq_send, gq_recv,
    d_send, d_recv, c_send, c_recv, a_send, a_recv, b_send, b_recv, r_send, r_recv, out_sem,
    dw_send, dw_recv, dz_send, dz_recv, dl_send, dl_recv,
):
    y, x, z, core = place()
    dp = 4 * y + x
    ctx = 2 * z + core
    mine = pick(core, x, y)
    other = pick(core, y, x)
    before, after = wrap(z - 1, 8), wrap(z + 1, 8)
    rows = q.shape[0]
    block = 2 * rows
    quarter = LATENT // 4
    piece = rows // 4
    two_kv = 2 * KV
    two_q = 2 * QK
    two_v = 2 * VDIM

    w_axis = lax.rem(z, 2)
    w_first = lax.rem(pick(w_axis, x, y) + 4 - z // 2, 4)
    w_other = pick(w_axis, y, x)
    part = block_at(mine, z)
    w_plane = 2 * part + core

    def dw_mate(plane):
        return line_dp(core, lax.rem(part + plane, 4), y, x), 2 * plane + core

    def dw_home(b):
        return 4 * other + z // 2, 2 * w_plane + b

    def dw_source(odd):
        plane = 2 * x + odd
        spot = lax.rem(z // 2 + plane, 4)
        return pick(w_axis, 4 * y + spot, 4 * spot + y), 2 * plane + w_axis

    def is_me(device):
        return (device[0] == dp) & (device[1] == ctx)

    def not_me(device):
        return jnp.logical_not(is_me(device))

    for d in range(16):
        there = lax.rem(dp + d, 16)
        if d:
            signal((there, ctx))
        signal((there, 2 * z + 1 - core))
    signal((dp, 2 * before + core))
    signal((dp, 2 * after + core))
    for d in range(1, 8):
        signal(dw_mate(lax.rem(z + d, 8)))
    strangers = 0
    for b in range(2):
        @pl.when(not_me((dp, 2 * w_plane + b)))
        def _():
            signal((dp, 2 * w_plane + b))

        @pl.when(not_me(dw_source(b)))
        def _():
            signal(dw_source(b))

        strangers += jnp.where(is_me((dp, 2 * (w_first + 4 * b) + w_axis)), 0, 1)
        strangers += jnp.where(is_me(dw_home(b)), 0, 1)

    pl.semaphore_wait(pltpu.get_barrier_semaphore(), 31 + 2 + 7 + strangers)

    moves = Sender()

    def w_home(i):
        return dp, 2 * (w_first + 4 * i) + w_axis

    def w_ends(k):
        src = w.at[pl.ds(pl.multiple_of(w_other * quarter, quarter), quarter), pl.ds(k * two_kv, two_kv)]
        return src, w_all.at[2 * core + k, w_other]

    def w_copy(k, i):
        src, dst = w_ends(k)
        return pltpu.make_async_remote_copy(
            src_ref=src, dst_ref=dst, send_sem=w_send.at[k, i], recv_sem=w_recv.at[2 * core + k],
            device_id=w_home(i), device_id_type=MESH,
        )

    def send_w(k):
        for i in range(2):
            @pl.when(is_me(w_home(i)))
            def _():
                src, dst = w_ends(k)
                pltpu.make_async_copy(src, dst, w_recv.at[2 * core + k]).start()

            @pl.when(not_me(w_home(i)))
            def _():
                w_copy(k, i).start()

    def share_w(pair):
        landed(w_all.at[pair, other], w_recv.at[pair])
        for d in range(1, 4):
            target = (line_dp(1 - core, lax.rem(other + d, 4), y, x), 2 * z + core)
            moves.remote(
                w_all.at[pair, other], w_all.at[pair, other], w_send2.at[pair, d], w_recv2.at[pair, d], target
            )

    def send_latent(d, e):
        axis = lax.rem(core + e, 2)
        spot = pick(axis, x, y)
        k = 4 * e + d
        dst = lat_all.at[spot, 2 + core]
        if d == 0 and e == 0:
            moves.local(latent, dst, l_recv.at[k])
        else:
            target = (line_dp(axis, lax.rem(spot + d, 4), y, x), 2 * z + axis)
            moves.remote(latent, dst, l_send.at[k], l_recv.at[k], target)

    def send_rows(pair, d, e):
        axis = lax.rem(core + e, 2)
        spot = pick(axis, x, y)
        there = lax.rem(spot + d, 4)
        target = (line_dp(axis, there, y, x), 2 * z + axis)
        k = 4 * e + d
        at = 4 * (2 * block_at(there, z) + axis) + pair
        q_part = q.at[:, pl.ds(pl.multiple_of(at * two_q, two_q), two_q)]
        g_part = g.at[:, pl.ds(pl.multiple_of(at * two_v, two_v), two_v)]
        q_dst, g_dst = q_all.at[pair, spot, core], g_all.at[pair, spot, core]
        if d == 0 and e == 0:
            moves.local(q_part, q_dst, recv.at[0, pair, k])
            moves.local(g_part, g_dst, recv.at[1, pair, k])
        else:
            moves.remote(q_part, q_dst, send.at[0, pair, k], recv.at[0, pair, k], target)
            moves.remote(g_part, g_dst, send.at[1, pair, k], recv.at[1, pair, k], target)

    def forward_latent(d):
        slot = wrap(mine - d, 4)
        for e in range(2):
            landed(lat_all.at[slot, 2 + lax.rem(core + e, 2)], l_recv.at[4 * e + d])
        moves.remote(
            lat_all.at[slot, pl.ds(2, 2)], lat_all.at[slot, pl.ds(0, 2)],
            z_send.at[0, d], z_recv.at[0, d], (dp, 2 * after + core),
        )

    send_w(0)
    for d in (0, 1, 3, 2):
        for e in range(2):
            send_latent(d, e)
    send_w(1)
    for d in (0, 1, 3, 2):
        for e in range(2):
            send_rows(0, d, e)
    d_acc[...] = jnp.zeros_like(d_acc)
    forward_latent(0)
    share_w(0)
    forward_latent(1)
    share_w(2)
    forward_latent(3)
    forward_latent(2)
    for d in (0, 1, 3, 2):
        for e in range(2):
            send_rows(2, d, e)
    share_w(1)
    share_w(3)
    for pair in (1, 3):
        for d in (0, 1, 3, 2):
            for e in range(2):
                send_rows(pair, d, e)
    p_t[...] = jnp.zeros_like(p_t)
    ds_t[...] = jnp.zeros_like(ds_t)

    def order(s):
        return s + (s // 2) * (1 - 2 * lax.rem(s, 2))

    def slot_of(s):
        return lax.rem(mine + 4 - order(s), 4)

    def pair_of(i):
        return 2 * lax.rem(i, 2) + i // 2

    def gq_copy(i, there, e, d, half):
        return pltpu.make_async_remote_copy(
            src_ref=gq.at[pair_of(i), :, half, pl.ds(pl.multiple_of(there * piece, piece), piece)],
            dst_ref=relay.at[i, core, pl.ds(4 * other, 4)],
            send_sem=gq_send.at[4 * e + d, i], recv_sem=gq_recv.at[4 * e + d, i],
            device_id=(line_dp(1 - core, there, y, x), 2 * z + half), device_id_type=MESH,
        )

    def relay_pair(i):
        for dm in (2, 1, 3, 0):
            there = lax.rem(other + dm, 4)
            for e in range(2):
                half = lax.rem(core + e, 2)
                if dm == 0 and e == 0:
                    src = gq.at[pair_of(i), :, half, pl.ds(pl.multiple_of(there * piece, piece), piece)]
                    pltpu.make_async_copy(src, relay.at[i, core, pl.ds(4 * other, 4)], gq_recv.at[0, i]).start()
                else:
                    gq_copy(i, there, e, dm, half).start()

    def r_copy(i, d):
        there = lax.rem(dp + d, 16)
        return pltpu.make_async_remote_copy(
            src_ref=chosen.at[i, there], dst_ref=come.at[i, dp], send_sem=r_send.at[i, d], recv_sem=r_recv.at[i, d],
            device_id=(there, ctx), device_id_type=MESH,
        )

    def deliver(i):
        for k in range(8):
            landed(relay.at[i, core, pl.ds(4 * other, 4)], gq_recv.at[k, i])
        relay_now[...] = relay[i]
        for d in (10, 2, 8, 6, 14, 9, 11, 1, 3, 4, 12, 5, 15, 7, 13, 0):
            there = lax.rem(dp + d, 16)
            chosen[i, there, 0] = relay_now[0, from_x[there]]
            chosen[i, there, 1] = relay_now[1, from_y[there]]
            if d == 0:
                pltpu.make_async_copy(chosen.at[i, there], come.at[i, dp], r_recv.at[i, d]).start()
            else:
                r_copy(i, d).start()

    def dw_copy(i, d):
        there = lax.rem(other + d, 4)
        return pltpu.make_async_remote_copy(
            src_ref=dw.at[i, there], dst_ref=dw_parts.at[i, other], send_sem=dw_send.at[i, d],
            recv_sem=dw_recv.at[i, d], device_id=(line_dp(1 - core, there, y, x), 2 * z + core), device_id_type=MESH,
        )

    def weight_first(i):
        dw[i] = dw_acc[...].astype(BF).reshape(4, quarter, two_kv)
        for d in (2, 1, 3, 0):
            if d == 0:
                pltpu.make_async_copy(dw.at[i, other], dw_parts.at[i, other], dw_recv.at[i, d]).start()
            else:
                dw_copy(i, d).start()

    def dz_copy(i, d):
        there = lax.rem(z + d, 8)
        return pltpu.make_async_remote_copy(
            src_ref=dw_total.at[i, there], dst_ref=dw_z.at[i, z], send_sem=dz_send.at[i, d],
            recv_sem=dz_recv.at[i, d], device_id=dw_mate(there), device_id_type=MESH,
        )

    def weight_second(i):
        for d in range(4):
            landed(dw_parts.at[i, wrap(other - d, 4)], dw_recv.at[i, d])
        total = dw_parts[i, 0].astype(F32)
        for n in range(1, 4):
            total += dw_parts[i, n].astype(F32)
        dw_total[i] = total.astype(BF).reshape(8, quarter // 8, two_kv)
        for d in (4, 3, 5, 2, 6, 1, 7, 0):
            if d == 0:
                pltpu.make_async_copy(dw_total.at[i, z], dw_z.at[i, z], dz_recv.at[i, d]).start()
            else:
                dz_copy(i, d).start()

    odd = lax.rem(z, 2)

    def last_ends(i):
        pair = pair_of(i)
        k = lax.rem(pair, 2)
        return dw_last.at[i], grad_w.at[odd, k], dl_recv.at[odd, k], dw_home(pair // 2)

    def last_copy(i):
        src, dst, sem, home = last_ends(i)
        return pltpu.make_async_remote_copy(
            src_ref=src, dst_ref=dst, send_sem=dl_send.at[i], recv_sem=sem, device_id=home, device_id_type=MESH
        )

    def weight_third(i):
        for d in range(8):
            landed(dw_z.at[i, wrap(z - d, 8)], dz_recv.at[i, d])
        total = dw_z[i, 0].astype(F32)
        for n in range(1, 8):
            total += dw_z[i, n].astype(F32)
        dw_last[i] = total
        src, dst, sem, home = last_ends(i)

        @pl.when(is_me(home))
        def _():
            pltpu.make_async_copy(src, dst, sem).start()

        @pl.when(not_me(home))
        def _():
            last_copy(i).start()

    def halo_copy(s, slot):
        return pltpu.make_async_remote_copy(
            src_ref=d_halo.at[slot], dst_ref=d_in.at[slot], send_sem=z_send.at[1, s], recv_sem=z_recv.at[1, s],
            device_id=(dp, 2 * before + core), device_id_type=MESH,
        )

    def d_copy(s, slot):
        return pltpu.make_async_remote_copy(
            src_ref=d_line.at[slot], dst_ref=d_lat.at[mine], send_sem=d_send.at[s], recv_sem=d_recv.at[s],
            device_id=(line_dp(core, slot, y, x), 2 * z + core), device_id_type=MESH,
        )

    def add_halo(s):
        slot = slot_of(s)
        landed(d_in.at[slot], z_recv.at[1, s])
        d_line[slot] = (d_acc[slot, block:] + d_in[slot].astype(F32)).astype(BF)

        @pl.when(s == 0)
        def _():
            pltpu.make_async_copy(d_line.at[slot], d_lat.at[mine], d_recv.at[s]).start()

        @pl.when(s > 0)
        def _():
            d_copy(s, slot).start()

    def step(n, _):
        i, s = n // 4, lax.rem(n, 4)
        pair = pair_of(i)
        d = order(s)
        slot = slot_of(s)

        @pl.when(s == 0)
        def _():
            dw_acc[...] = jnp.zeros_like(dw_acc)
            for dm in range(1, 4):
                landed(w_all.at[pair, wrap(other - dm, 4)], w_recv2.at[pair, dm])

        @pl.when(i == 0)
        def _():
            landed(lat_all.at[slot, pl.ds(0, 2)], z_recv.at[0, d])

        for e in range(2):
            half = lax.rem(core + e, 2)
            landed(q_all.at[pair, slot, half], recv.at[0, pair, 4 * e + d])
            landed(g_all.at[pair, slot, half], recv.at[1, pair, 4 * e + d])
        heads(slot, pair, lo, q_all, g_all, lat_all, w_all, gq, d_acc, dw_acc, p_t, ds_t)

        @pl.when(i == 3)
        def _():
            d_halo[slot] = d_acc[slot, :block].astype(BF)
            halo_copy(s, slot).start()

            @pl.when(s > 0)
            def _():
                add_halo(s - 1)

        @pl.when(s == 3)
        def _():
            relay_pair(i)
            weight_first(i)

        @pl.when((s == 2) & (i > 0))
        def _():
            deliver(i - 1)
            weight_second(i - 1)

        @pl.when((s == 2) & (i > 1))
        def _():
            weight_third(i - 2)

        return 0

    lax.fori_loop(0, 16, step, 0)

    three = jnp.int32(3)
    add_halo(three)
    deliver(three)
    weight_second(three)

    def collect(s, _):
        landed(d_lat.at[lax.rem(mine + order(s), 4)], d_recv.at[s])
        return 0

    lax.fori_loop(0, 4, collect, 0)
    total = d_lat[0].astype(F32)
    for i in range(1, 4):
        total += d_lat[i].astype(F32)
    d_sum[...] = total.reshape(d_sum.shape)
    moves.remote(d_sum.at[1 - core], d_cross, c_send, c_recv, (dp, 2 * z + 1 - core))
    weight_third(jnp.int32(2))
    landed(d_cross, c_recv)
    d_sum[core] += d_cross[...]
    for d in range(16):
        there = lax.rem(dp + d, 16)
        if d == 0:
            moves.local(d_sum.at[core, there], d_relay.at[dp], a_recv.at[d])
        else:
            moves.remote(d_sum.at[core, there], d_relay.at[dp], a_send.at[d], a_recv.at[d], (there, ctx))

    def put(i):
        for d in range(15, -1, -1):
            source = wrap(dp - d, 16)
            landed(come.at[i, source], r_recv.at[i, d])
            sy, sx = source // 4, lax.rem(source, 4)
            for j, at, row in ((0, 8 * block_at(sx, z), sy), (1, 8 * block_at(sy, z) + 4, sx)):
                dst = grad_q.at[
                    pl.ds(pl.multiple_of(row * piece, piece), piece),
                    pl.ds(pl.multiple_of((at + pair_of(i)) * two_q, two_q), two_q),
                ]
                pltpu.make_async_copy(come.at[i, source, j], dst, out_sem).start()

    def put_early(i, _):
        put(i)
        return 0

    lax.fori_loop(0, 3, put_early, 0)
    for d in range(16):
        landed(d_relay.at[dp], a_recv.at[d])
    for d in range(16):
        there = lax.rem(dp + d, 16)
        d_pick[there] = d_relay[from_x[there]]
        if d == 0:
            moves.local(d_pick.at[there], grad_lat.at[dp], b_recv.at[d])
        else:
            moves.remote(d_pick.at[there], grad_lat.at[dp], b_send.at[d], b_recv.at[d], (there, ctx))
    weight_third(three)
    put(three)

    for d in range(16):
        landed(d_pick.at[dp], b_recv.at[d])
    for b in range(2):
        for k in range(2):
            landed(dw_last.at[0], dl_recv.at[b, k])

            @pl.when(not_me(w_home(b)))
            def _():
                w_copy(k, b).wait_send()

    for copy in moves.sent:
        copy.wait_send()

    def close(i, _):
        for k in range(1, 8):
            landed(relay.at[i, core, pl.ds(4 * other, 4)], gq_send.at[k, i])
        for d in range(1, 16):
            r_copy(i, d).wait_send()
        for d in range(1, 4):
            dw_copy(i, d).wait_send()
        for d in range(1, 8):
            dz_copy(i, d).wait_send()

        @pl.when(not_me(dw_home(pair_of(i) // 2)))
        def _():
            last_copy(i).wait_send()

        slot = slot_of(i)
        landed(d_halo.at[slot], z_send.at[1, i])

        @pl.when(i > 0)
        def _():
            landed(d_line.at[slot], d_send.at[i])

        return 0

    lax.fori_loop(0, 4, close, 0)
    landed(grad_q, out_sem)


def main_part(lo, from_x, from_y, q, latent, w, g):
    rows = q.shape[0]
    block, window = 2 * rows, 4 * rows
    quarter = LATENT // 4
    two_q, two_v, two_kv = 2 * QK, 2 * VDIM, 2 * KV
    dma = pltpu.SemaphoreType.DMA
    vmem = pl.BlockSpec(memory_space=pltpu.VMEM)
    smem = pl.BlockSpec(memory_space=pltpu.SMEM)
    return pl.pallas_call(
        main_kernel,
        out_shape=[
            jax.ShapeDtypeStruct(q.shape, BF),
            jax.ShapeDtypeStruct((16, rows // 16, WIDE), F32),
            jax.ShapeDtypeStruct((2, 2, quarter // 8, two_kv), F32),
        ],
        in_specs=[vmem, smem, smem] + [ANY] * 4,
        out_specs=[ANY] * 3,
        scratch_shapes=[
            pltpu.VMEM((4, 4, 2, rows, two_q), BF),
            pltpu.VMEM((4, 4, 2, rows, two_v), BF),
            pltpu.VMEM((4, 4, rows, WIDE), BF),
            pltpu.VMEM((4, 4, quarter, two_kv), BF),
            pltpu.VMEM((4, 4, 2, rows, two_q), BF),
            pltpu.VMEM((4, 2, 16, rows // 4, two_q), BF),
            pltpu.VMEM((2, 16, rows // 4, two_q), BF),
            pltpu.VMEM((4, 16, 2, rows // 4, two_q), BF),
            pltpu.VMEM((4, 16, 2, rows // 4, two_q), BF),
            pltpu.VMEM((4, window, WIDE), F32),
            pltpu.VMEM((4, block, WIDE), BF),
            pltpu.VMEM((4, block, WIDE), BF),
            pltpu.VMEM((4, block, WIDE), BF),
            pltpu.VMEM((4, block, WIDE), BF),
            pltpu.VMEM((2, 16, rows // 16, WIDE), F32),
            pltpu.VMEM((16, rows // 16, WIDE), F32),
            pltpu.VMEM((16, rows // 16, WIDE), F32),
            pltpu.VMEM((16, rows // 16, WIDE), F32),
            pltpu.VMEM((4, 4, quarter, two_kv), BF),
            pltpu.VMEM((4, 4, quarter, two_kv), BF),
            pltpu.VMEM((4, 8, quarter // 8, two_kv), BF),
            pltpu.VMEM((4, 8, quarter // 8, two_kv), BF),
            pltpu.VMEM((4, quarter // 8, two_kv), F32),
            pltpu.VMEM((LATENT, two_kv), F32),
            pltpu.VMEM((2, window, block), BF),
            pltpu.VMEM((2, window, block), BF),
            dma((2, 4, 8)), dma((2, 4, 8)), dma((8,)), dma((8,)), dma((2, 2)), dma((4,)), dma((4, 4)), dma((4, 4)),
            dma((2, 4)), dma((2, 4)), dma((8, 4)), dma((8, 4)), dma((4,)), dma((4,)), dma, dma,
            dma((16,)), dma((16,)), dma((16,)), dma((16,)), dma((4, 16)), dma((4, 16)), dma,
            dma((4, 4)), dma((4, 4)), dma((4, 8)), dma((4, 8)), dma((4,)), dma((2, 2)),
        ],
        compiler_params=pltpu.CompilerParams(
            collective_id=0, has_side_effects=True, vmem_limit_bytes=60 * 1024 * 1024
        ),
        name="heads_and_exchanges",
    )(lo, from_x, from_y, q, latent, w, g)


def body(queries, latent, w_kv, grad_out, doc_lengths, matching):
    y, x, z, core = place()
    dp = 4 * y + x
    rows = queries.shape[0]
    block = 2 * rows

    packs = pick(core, 4 * y + jnp.arange(4), 4 * jnp.arange(4) + x)
    ends = jnp.cumsum(doc_lengths[packs], axis=1)
    token = z * block + jnp.arange(block, dtype=jnp.int32)
    begun = jnp.where(ends[:, None, :] <= token[None, :, None], ends[:, None, :], 0)
    lo = (jnp.max(begun, axis=2) - (z - 1) * block)[:, None, :].astype(jnp.int32)

    turned = 4 * lax.rem(matching, 4) + matching // 4
    grad_queries, grad_latent, grad_weight = main_part(lo, matching, turned, queries, latent, w_kv, grad_out)
    return grad_queries, grad_latent.reshape(rows, WIDE), grad_weight.transpose(0, 2, 1, 3).reshape(LATENT // 16, -1)


def solution(mesh):
    in_specs = (
        P(("dp", "ctx"), None),
        P(("dp", "ctx"), None),
        P(None, "ctx"),
        P(("dp", "ctx"), None),
        P(),
        P(),
    )
    out_specs = (P(("dp", "ctx"), None), P(("dp", "ctx"), None), P("dp", "ctx"))
    return jax.shard_map(body, mesh=mesh, in_specs=in_specs, out_specs=out_specs, check_vma=False)
```

```python
import jax
import jax.numpy as jnp
from jax import lax
from jax.experimental import pallas as pl
from jax.experimental.pallas import tpu as pltpu
from jax.sharding import PartitionSpec as P

NOPE = 128
ROPE = 64
VDIM = 128
LATENT = 512
HEADS = 64
ROWS = 128
QK = NOPE + ROPE
KV = NOPE + VDIM
WIDE = LATENT + ROPE
MESH = pl.DeviceIdType.MESH
ANY = pl.BlockSpec(memory_space=pl.ANY)
BF = jnp.bfloat16
F32 = jnp.float32
LOW = -1e30


def place():
    dp, ctx = lax.axis_index("dp"), lax.axis_index("ctx")
    return dp // 4, lax.rem(dp, 4), ctx // 2, lax.rem(ctx, 2)


def pick(axis, on_x, on_y):
    return (1 - axis) * on_x + axis * on_y


def wrap(value, n):
    return lax.rem(value + n, n)


def line_dp(axis, position, y, x):
    return pick(axis, 4 * y + position, 4 * position + x)


class Sender:
    def __init__(self):
        self.sent = []
        self.due = []

    def remote(self, src, dst, send_sem, recv_sem, device):
        copy = pltpu.make_async_remote_copy(
            src_ref=src, dst_ref=dst, send_sem=send_sem, recv_sem=recv_sem,
            device_id=device, device_id_type=MESH,
        )
        copy.start()
        self.sent.append(copy)
        return copy

    def local(self, src, dst, sem):
        copy = pltpu.make_async_copy(src, dst, sem)
        copy.start()
        self.due.append(copy)


def signal(device):
    pl.semaphore_signal(pltpu.get_barrier_semaphore(), inc=1, device_id=device, device_id_type=MESH)


def block_at(position, z):
    return lax.rem(position + 8 - z, 4)


def landed(ref, sem):
    pltpu.make_async_copy(ref, ref, sem).wait()


def nt(a, b):
    return lax.dot_general(a, b, (((1,), (1,)), ((), ())), preferred_element_type=F32)


def tn(a, b):
    return lax.dot_general(a, b, (((0,), (0,)), ((), ())), preferred_element_type=F32)


def nn(a, b):
    return jnp.dot(a, b, preferred_element_type=F32)


def heads(t, pair, lo, q, g, lat, w, gq, d_acc, dw_acc, p_t, ds_t):
    rows = q.shape[3]
    block = 2 * rows
    window = 4 * rows
    scale = float(QK) ** -0.5

    nope = lat[t, :, :, :LATENT].reshape(window, LATENT)
    rope = lat[t, :, :, LATENT:].reshape(window, ROPE)
    w_two = w[pair]
    lows = lo[t]
    key_at = lax.broadcasted_iota(jnp.int32, (3 * rows, rows), 0)
    query_at = lax.broadcasted_iota(jnp.int32, (3 * rows, rows), 1)
    kv_two = nn(nope, w_two).astype(BF)
    q_two = q[pair, t].reshape(block, 2 * QK)
    g_two = g[pair, t].reshape(block, 2 * VDIM)
    dq_two, dkv_two = [], []
    d_rope = None
    for h in range(2):
        qh = q_two[:, h * QK:(h + 1) * QK]
        gh = g_two[:, h * VDIM:(h + 1) * VDIM]
        kh = jnp.concatenate([kv_two[:, h * KV:h * KV + NOPE], rope], axis=1)
        vh = kv_two[:, h * KV + NOPE:(h + 1) * KV]
        scores = nt(kh, qh)
        dprobs = nt(vh, gh)
        for s in range(2):
            keys = slice(rows * s, rows * s + 3 * rows)
            queries = slice(rows * s, rows * s + rows)
            low = lows[:, queries] - rows * s
            seen = (key_at >= low) & (key_at <= query_at + block)
            sc = jnp.where(seen, scores[keys, queries] * scale, LOW)
            top = jnp.max(sc, axis=0, keepdims=True)
            ex = jnp.exp(sc - top)
            probs = ex * (1.0 / jnp.sum(ex, axis=0, keepdims=True))
            probs_low = probs.astype(BF)
            dp = dprobs[keys, queries]
            row_dot = jnp.sum(probs_low.astype(F32) * dp, axis=0, keepdims=True)
            p_t[h, keys, queries] = probs_low
            ds_t[h, keys, queries] = (probs * (dp - row_dot)).astype(BF)
        ds = ds_t[h]
        dq_two.append((tn(ds, kh) * scale).astype(BF))
        dk = nn(ds, qh) * scale
        dv = nn(p_t[h], gh)
        d_rope = dk[:, NOPE:] if d_rope is None else d_rope + dk[:, NOPE:]
        dkv_two += [dk[:, :NOPE].astype(BF), dv.astype(BF)]
    gkv = jnp.concatenate(dkv_two, axis=1)
    gq[pair, t] = jnp.concatenate(dq_two, axis=1).reshape(2, rows, 2 * QK)
    d_acc[t, :, :LATENT] += nt(gkv, w_two)
    d_acc[t, :, LATENT:] += d_rope
    dw_acc[...] += tn(nope, gkv)


def main_kernel(
    lengths, matching, q, latent, w, g,
    grad_q, grad_lat, grad_w,
    lo, q_all, g_all, lat_all, w_all, gq, relay, relay_now, chosen, come,
    d_acc, d_halo, d_in, d_line, d_lat, d_sum, d_cross, d_relay, d_pick,
    dw, dw_parts, dw_total, dw_z, dw_last, dw_acc, p_t, ds_t,
    send, recv, l_send, l_recv, w_send, w_recv, w_send2, w_recv2, z_send, z_recv, gq_send, gq_recv,
    d_send, d_recv, c_send, c_recv, a_send, a_recv, b_send, b_recv, r_send, r_recv, out_sem,
    dw_send, dw_recv, dz_send, dz_recv, dl_send, dl_recv,
):
    y, x, z, core = place()
    dp = 4 * y + x
    ctx = 2 * z + core
    mine = pick(core, x, y)
    other = pick(core, y, x)
    before, after = wrap(z - 1, 8), wrap(z + 1, 8)
    rows = q.shape[0]
    block = 2 * rows
    quarter = LATENT // 4
    piece = rows // 4
    two_kv = 2 * KV
    two_q = 2 * QK
    two_v = 2 * VDIM

    w_axis = lax.rem(z, 2)
    w_first = lax.rem(pick(w_axis, x, y) + 4 - z // 2, 4)
    w_other = pick(w_axis, y, x)
    part = block_at(mine, z)
    w_plane = 2 * part + core

    def dw_mate(plane):
        return line_dp(core, lax.rem(part + plane, 4), y, x), 2 * plane + core

    def dw_home(b):
        return 4 * other + z // 2, 2 * w_plane + b

    def dw_source(odd):
        plane = 2 * x + odd
        spot = lax.rem(z // 2 + plane, 4)
        return pick(w_axis, 4 * y + spot, 4 * spot + y), 2 * plane + w_axis

    def is_me(device):
        return (device[0] == dp) & (device[1] == ctx)

    def not_me(device):
        return jnp.logical_not(is_me(device))

    for d in range(16):
        there = lax.rem(dp + d, 16)
        if d:
            signal((there, ctx))
        signal((there, 2 * z + 1 - core))
    signal((dp, 2 * before + core))
    signal((dp, 2 * after + core))
    for d in range(1, 8):
        signal(dw_mate(lax.rem(z + d, 8)))
    strangers = 0
    for b in range(2):
        @pl.when(not_me((dp, 2 * w_plane + b)))
        def _():
            signal((dp, 2 * w_plane + b))

        @pl.when(not_me(dw_source(b)))
        def _():
            signal(dw_source(b))

        strangers += jnp.where(is_me((dp, 2 * (w_first + 4 * b) + w_axis)), 0, 1)
        strangers += jnp.where(is_me(dw_home(b)), 0, 1)

    pl.semaphore_wait(pltpu.get_barrier_semaphore(), 31 + 2 + 7 + strangers)

    moves = Sender()

    def w_home(i):
        return dp, 2 * (w_first + 4 * i) + w_axis

    def w_part(pair, at):
        return w_all.at[pair, pl.ds(pl.multiple_of(at * quarter, quarter), quarter)]

    def w_ends(k):
        src = w.at[pl.ds(pl.multiple_of(w_other * quarter, quarter), quarter), pl.ds(k * two_kv, two_kv)]
        return src, w_part(2 * core + k, w_other)

    def w_copy(k, i):
        src, dst = w_ends(k)
        return pltpu.make_async_remote_copy(
            src_ref=src, dst_ref=dst, send_sem=w_send.at[k, i], recv_sem=w_recv.at[2 * core + k],
            device_id=w_home(i), device_id_type=MESH,
        )

    def send_w(k):
        for i in range(2):
            @pl.when(is_me(w_home(i)))
            def _():
                src, dst = w_ends(k)
                pltpu.make_async_copy(src, dst, w_recv.at[2 * core + k]).start()

            @pl.when(not_me(w_home(i)))
            def _():
                w_copy(k, i).start()

    def share_w(pair):
        landed(w_part(pair, other), w_recv.at[pair])
        for d in range(1, 4):
            target = (line_dp(1 - core, lax.rem(other + d, 4), y, x), 2 * z + core)
            moves.remote(
                w_part(pair, other), w_part(pair, other), w_send2.at[pair, d], w_recv2.at[pair, d], target
            )

    def send_latent(d, e):
        axis = lax.rem(core + e, 2)
        spot = pick(axis, x, y)
        k = 4 * e + d
        dst = lat_all.at[spot, 2 + core]
        if d == 0 and e == 0:
            moves.local(latent, dst, l_recv.at[k])
        else:
            target = (line_dp(axis, lax.rem(spot + d, 4), y, x), 2 * z + axis)
            moves.remote(latent, dst, l_send.at[k], l_recv.at[k], target)

    def send_rows(pair, d, e):
        axis = lax.rem(core + e, 2)
        spot = pick(axis, x, y)
        there = lax.rem(spot + d, 4)
        target = (line_dp(axis, there, y, x), 2 * z + axis)
        k = 4 * e + d
        at = 4 * (2 * block_at(there, z) + axis) + pair
        q_part = q.at[:, pl.ds(pl.multiple_of(at * two_q, two_q), two_q)]
        g_part = g.at[:, pl.ds(pl.multiple_of(at * two_v, two_v), two_v)]
        q_dst, g_dst = q_all.at[pair, spot, core], g_all.at[pair, spot, core]
        if d == 0 and e == 0:
            moves.local(q_part, q_dst, recv.at[0, pair, k])
            moves.local(g_part, g_dst, recv.at[1, pair, k])
        else:
            moves.remote(q_part, q_dst, send.at[0, pair, k], recv.at[0, pair, k], target)
            moves.remote(g_part, g_dst, send.at[1, pair, k], recv.at[1, pair, k], target)

    def forward_latent(d):
        slot = wrap(mine - d, 4)
        for e in range(2):
            landed(lat_all.at[slot, 2 + lax.rem(core + e, 2)], l_recv.at[4 * e + d])
        moves.remote(
            lat_all.at[slot, pl.ds(2, 2)], lat_all.at[slot, pl.ds(0, 2)],
            z_send.at[0, d], z_recv.at[0, d], (dp, 2 * after + core),
        )

    send_w(0)
    for d in (0, 1, 3, 2):
        for e in range(2):
            send_latent(d, e)
    send_w(1)
    for d in (0, 1, 3, 2):
        for e in range(2):
            send_rows(0, d, e)
    d_acc[...] = jnp.zeros_like(d_acc)
    forward_latent(0)
    share_w(0)
    forward_latent(1)
    share_w(2)
    forward_latent(3)
    forward_latent(2)
    for d in (0, 1, 3, 2):
        for e in range(2):
            send_rows(2, d, e)
    share_w(1)
    share_w(3)
    for pair in (1, 3):
        for d in (0, 1, 3, 2):
            for e in range(2):
                send_rows(pair, d, e)
    p_t[...] = jnp.zeros_like(p_t)
    ds_t[...] = jnp.zeros_like(ds_t)

    token = z * block + lax.broadcasted_iota(jnp.int32, (1, block), 1)
    for slot in range(4):
        pack = pick(core, 4 * y + slot, 4 * slot + x)
        end = jnp.int32(0)
        begun = jnp.zeros((1, block), jnp.int32)
        for k in range(lengths.shape[1]):
            end = end + lengths[pack, k]
            begun = jnp.where(token >= end, end, begun)
        lo[slot] = begun - (z - 1) * block

    def order(s):
        return s + (s // 2) * (1 - 2 * lax.rem(s, 2))

    def slot_of(s):
        return lax.rem(mine + 4 - order(s), 4)

    def pair_of(i):
        return 2 * lax.rem(i, 2) + i // 2

    def gq_copy(i, there, e, d, half):
        return pltpu.make_async_remote_copy(
            src_ref=gq.at[pair_of(i), :, half, pl.ds(pl.multiple_of(there * piece, piece), piece)],
            dst_ref=relay.at[i, core, pl.ds(4 * other, 4)],
            send_sem=gq_send.at[4 * e + d, i], recv_sem=gq_recv.at[4 * e + d, i],
            device_id=(line_dp(1 - core, there, y, x), 2 * z + half), device_id_type=MESH,
        )

    def relay_pair(i):
        for dm in (2, 1, 3, 0):
            there = lax.rem(other + dm, 4)
            for e in range(2):
                half = lax.rem(core + e, 2)
                if dm == 0 and e == 0:
                    src = gq.at[pair_of(i), :, half, pl.ds(pl.multiple_of(there * piece, piece), piece)]
                    pltpu.make_async_copy(src, relay.at[i, core, pl.ds(4 * other, 4)], gq_recv.at[0, i]).start()
                else:
                    gq_copy(i, there, e, dm, half).start()

    def ahead(d):
        return 4 * lax.rem(y + d // 4, 4) + lax.rem(x + d % 4, 4)

    def behind(d):
        return 4 * wrap(y - d // 4, 4) + wrap(x - d % 4, 4)

    def r_copy(i, d):
        there = ahead(d)
        return pltpu.make_async_remote_copy(
            src_ref=chosen.at[i, there], dst_ref=come.at[i, dp], send_sem=r_send.at[i, d], recv_sem=r_recv.at[i, d],
            device_id=(there, ctx), device_id_type=MESH,
        )

    def deliver(i):
        for k in range(8):
            landed(relay.at[i, core, pl.ds(4 * other, 4)], gq_recv.at[k, i])
        relay_now[...] = relay[i]
        for d in (10, 2, 8, 1, 3, 4, 12, 5, 15, 7, 13, 6, 14, 9, 11, 0):
            there = ahead(d)
            pack = matching[there]
            chosen[i, there, 0] = relay_now[0, pack]
            chosen[i, there, 1] = relay_now[1, 4 * lax.rem(pack, 4) + pack // 4]
            if d == 0:
                pltpu.make_async_copy(chosen.at[i, there], come.at[i, dp], r_recv.at[i, d]).start()
            else:
                r_copy(i, d).start()

    def dw_copy(i, d):
        there = lax.rem(other + d, 4)
        return pltpu.make_async_remote_copy(
            src_ref=dw.at[i, there], dst_ref=dw_parts.at[i, other], send_sem=dw_send.at[i, d],
            recv_sem=dw_recv.at[i, d], device_id=(line_dp(1 - core, there, y, x), 2 * z + core), device_id_type=MESH,
        )

    def weight_first(i):
        dw[i] = dw_acc[lax.rem(i, 2)].astype(BF).reshape(4, quarter, two_kv)
        for d in (2, 1, 3, 0):
            if d == 0:
                pltpu.make_async_copy(dw.at[i, other], dw_parts.at[i, other], dw_recv.at[i, d]).start()
            else:
                dw_copy(i, d).start()

    def dz_copy(i, d):
        there = lax.rem(z + d, 8)
        return pltpu.make_async_remote_copy(
            src_ref=dw_total.at[i, there], dst_ref=dw_z.at[i, z], send_sem=dz_send.at[i, d],
            recv_sem=dz_recv.at[i, d], device_id=dw_mate(there), device_id_type=MESH,
        )

    def weight_second(i):
        for d in range(4):
            landed(dw_parts.at[i, wrap(other - d, 4)], dw_recv.at[i, d])
        total = dw_parts[i, 0].astype(F32)
        for n in range(1, 4):
            total += dw_parts[i, n].astype(F32)
        dw_total[i] = total.astype(BF).reshape(8, quarter // 8, two_kv)
        for d in (4, 3, 5, 2, 6, 1, 7, 0):
            if d == 0:
                pltpu.make_async_copy(dw_total.at[i, z], dw_z.at[i, z], dz_recv.at[i, d]).start()
            else:
                dz_copy(i, d).start()

    odd = lax.rem(z, 2)

    def last_ends(i):
        pair = pair_of(i)
        k = lax.rem(pair, 2)
        return dw_last.at[i], grad_w.at[odd, k], dl_recv.at[odd, k], dw_home(pair // 2)

    def last_copy(i):
        src, dst, sem, home = last_ends(i)
        return pltpu.make_async_remote_copy(
            src_ref=src, dst_ref=dst, send_sem=dl_send.at[i], recv_sem=sem, device_id=home, device_id_type=MESH
        )

    def weight_third(i):
        for d in range(8):
            landed(dw_z.at[i, wrap(z - d, 8)], dz_recv.at[i, d])
        total = dw_z[i, 0].astype(F32)
        for n in range(1, 8):
            total += dw_z[i, n].astype(F32)
        dw_last[i] = total
        src, dst, sem, home = last_ends(i)

        @pl.when(is_me(home))
        def _():
            pltpu.make_async_copy(src, dst, sem).start()

        @pl.when(not_me(home))
        def _():
            last_copy(i).start()

    def halo_copy(s, slot):
        return pltpu.make_async_remote_copy(
            src_ref=d_halo.at[slot], dst_ref=d_in.at[slot], send_sem=z_send.at[1, s], recv_sem=z_recv.at[1, s],
            device_id=(dp, 2 * before + core), device_id_type=MESH,
        )

    def d_copy(s, slot):
        return pltpu.make_async_remote_copy(
            src_ref=d_line.at[slot], dst_ref=d_lat.at[mine], send_sem=d_send.at[s], recv_sem=d_recv.at[s],
            device_id=(line_dp(core, slot, y, x), 2 * z + core), device_id_type=MESH,
        )

    def add_halo(s):
        slot = slot_of(s)
        landed(d_in.at[slot], z_recv.at[1, s])
        d_line[slot] = (d_acc[slot, block:] + d_in[slot].astype(F32)).astype(BF)

        @pl.when(s == 0)
        def _():
            pltpu.make_async_copy(d_line.at[slot], d_lat.at[mine], d_recv.at[s]).start()

        @pl.when(s > 0)
        def _():
            d_copy(s, slot).start()

    def step(n, _):
        early = jnp.where(n < 8, 1, 0)
        i = early * lax.rem(n, 2) + (1 - early) * (n // 4)
        s = early * (n // 2) + (1 - early) * lax.rem(n, 4)
        pair = pair_of(i)
        d = order(s)
        slot = slot_of(s)

        @pl.when(s == 0)
        def _():
            dw_acc[lax.rem(i, 2)] = jnp.zeros(dw_acc.shape[1:], F32)

        @pl.when(s == 0)
        def _():
            for dm in range(1, 4):
                landed(w_part(pair, wrap(other - dm, 4)), w_recv2.at[pair, dm])

        @pl.when(i == 0)
        def _():
            landed(lat_all.at[slot, pl.ds(0, 2)], z_recv.at[0, d])

        for e in range(2):
            half = lax.rem(core + e, 2)
            landed(q_all.at[pair, slot, half], recv.at[0, pair, 4 * e + d])
            landed(g_all.at[pair, slot, half], recv.at[1, pair, 4 * e + d])
        heads(slot, pair, lo, q_all, g_all, lat_all, w_all, gq, d_acc, dw_acc.at[lax.rem(i, 2)], p_t, ds_t)

        @pl.when(i == 3)
        def _():
            d_halo[slot] = d_acc[slot, :block].astype(BF)
            halo_copy(s, slot).start()

            @pl.when(s > 0)
            def _():
                add_halo(s - 1)

        @pl.when(s == 3)
        def _():
            relay_pair(i)
            weight_first(i)

        @pl.when((n == 9) | (n == 10) | (n == 14))
        def _():
            done = jnp.where(n == 14, 2, n - 9)
            deliver(done)
            weight_second(done)

        @pl.when((n == 12) | (n == 13))
        def _():
            weight_third(n - 12)

        return 0

    lax.fori_loop(0, 16, step, 0)

    three = jnp.int32(3)
    add_halo(three)
    deliver(three)
    weight_second(three)

    def collect(s, _):
        landed(d_lat.at[lax.rem(mine + order(s), 4)], d_recv.at[s])
        return 0

    lax.fori_loop(0, 4, collect, 0)
    total = d_lat[0].astype(F32)
    for i in range(1, 4):
        total += d_lat[i].astype(F32)
    d_sum[...] = total.reshape(d_sum.shape)
    moves.remote(d_sum.at[1 - core], d_cross, c_send, c_recv, (dp, 2 * z + 1 - core))
    weight_third(jnp.int32(2))
    landed(d_cross, c_recv)
    d_sum[core] += d_cross[...]
    for d in range(16):
        there = ahead(d)
        if d == 0:
            moves.local(d_sum.at[core, there], d_relay.at[dp], a_recv.at[d])
        else:
            moves.remote(d_sum.at[core, there], d_relay.at[dp], a_send.at[d], a_recv.at[d], (there, ctx))

    def put(i):
        for d in range(15, -1, -1):
            source = behind(d)
            landed(come.at[i, source], r_recv.at[i, d])
            sy, sx = source // 4, lax.rem(source, 4)
            for j, at, row in ((0, 8 * block_at(sx, z), sy), (1, 8 * block_at(sy, z) + 4, sx)):
                dst = grad_q.at[
                    pl.ds(pl.multiple_of(row * piece, piece), piece),
                    pl.ds(pl.multiple_of((at + pair_of(i)) * two_q, two_q), two_q),
                ]
                pltpu.make_async_copy(come.at[i, source, j], dst, out_sem).start()

    def put_early(i, _):
        put(i)
        return 0

    lax.fori_loop(0, 3, put_early, 0)
    for d in range(16):
        landed(d_relay.at[dp], a_recv.at[d])
    for d in range(16):
        there = ahead(d)
        d_pick[there] = d_relay[matching[there]]
        if d == 0:
            moves.local(d_pick.at[there], grad_lat.at[dp], b_recv.at[d])
        else:
            moves.remote(d_pick.at[there], grad_lat.at[dp], b_send.at[d], b_recv.at[d], (there, ctx))
    weight_third(three)
    put(three)

    for d in range(16):
        landed(d_pick.at[dp], b_recv.at[d])
    for b in range(2):
        for k in range(2):
            landed(dw_last.at[0], dl_recv.at[b, k])

            @pl.when(not_me(w_home(b)))
            def _():
                w_copy(k, b).wait_send()

    for copy in moves.sent:
        copy.wait_send()

    def close(i, _):
        for k in range(1, 8):
            landed(relay.at[i, core, pl.ds(4 * other, 4)], gq_send.at[k, i])
        for d in range(1, 16):
            r_copy(i, d).wait_send()
        for d in range(1, 4):
            dw_copy(i, d).wait_send()
        for d in range(1, 8):
            dz_copy(i, d).wait_send()

        @pl.when(not_me(dw_home(pair_of(i) // 2)))
        def _():
            last_copy(i).wait_send()

        slot = slot_of(i)
        landed(d_halo.at[slot], z_send.at[1, i])

        @pl.when(i > 0)
        def _():
            landed(d_line.at[slot], d_send.at[i])

        return 0

    lax.fori_loop(0, 4, close, 0)
    landed(grad_q, out_sem)


def main_part(lengths, matching, q, latent, w, g):
    rows = q.shape[0]
    block, window = 2 * rows, 4 * rows
    quarter = LATENT // 4
    two_q, two_v, two_kv = 2 * QK, 2 * VDIM, 2 * KV
    dma = pltpu.SemaphoreType.DMA
    smem = pl.BlockSpec(memory_space=pltpu.SMEM)
    return pl.pallas_call(
        main_kernel,
        out_shape=[
            jax.ShapeDtypeStruct(q.shape, BF),
            jax.ShapeDtypeStruct((16, rows // 16, WIDE), F32),
            jax.ShapeDtypeStruct((2, 2, quarter // 8, two_kv), F32),
        ],
        in_specs=[smem, smem] + [ANY] * 4,
        out_specs=[ANY] * 3,
        scratch_shapes=[
            pltpu.VMEM((4, 1, block), jnp.int32),
            pltpu.VMEM((4, 4, 2, rows, two_q), BF),
            pltpu.VMEM((4, 4, 2, rows, two_v), BF),
            pltpu.VMEM((4, 4, rows, WIDE), BF),
            pltpu.VMEM((4, LATENT, two_kv), BF),
            pltpu.VMEM((4, 4, 2, rows, two_q), BF),
            pltpu.VMEM((4, 2, 16, rows // 4, two_q), BF),
            pltpu.VMEM((2, 16, rows // 4, two_q), BF),
            pltpu.VMEM((4, 16, 2, rows // 4, two_q), BF),
            pltpu.VMEM((4, 16, 2, rows // 4, two_q), BF),
            pltpu.VMEM((4, window, WIDE), F32),
            pltpu.VMEM((4, block, WIDE), BF),
            pltpu.VMEM((4, block, WIDE), BF),
            pltpu.VMEM((4, block, WIDE), BF),
            pltpu.VMEM((4, block, WIDE), BF),
            pltpu.VMEM((2, 16, rows // 16, WIDE), F32),
            pltpu.VMEM((16, rows // 16, WIDE), F32),
            pltpu.VMEM((16, rows // 16, WIDE), F32),
            pltpu.VMEM((16, rows // 16, WIDE), F32),
            pltpu.VMEM((4, 4, quarter, two_kv), BF),
            pltpu.VMEM((4, 4, quarter, two_kv), BF),
            pltpu.VMEM((4, 8, quarter // 8, two_kv), BF),
            pltpu.VMEM((4, 8, quarter // 8, two_kv), BF),
            pltpu.VMEM((4, quarter // 8, two_kv), F32),
            pltpu.VMEM((2, LATENT, two_kv), F32),
            pltpu.VMEM((2, window, block), BF),
            pltpu.VMEM((2, window, block), BF),
            dma((2, 4, 8)), dma((2, 4, 8)), dma((8,)), dma((8,)), dma((2, 2)), dma((4,)), dma((4, 4)), dma((4, 4)),
            dma((2, 4)), dma((2, 4)), dma((8, 4)), dma((8, 4)), dma((4,)), dma((4,)), dma, dma,
            dma((16,)), dma((16,)), dma((16,)), dma((16,)), dma((4, 16)), dma((4, 16)), dma,
            dma((4, 4)), dma((4, 4)), dma((4, 8)), dma((4, 8)), dma((4,)), dma((2, 2)),
        ],
        compiler_params=pltpu.CompilerParams(
            collective_id=0, has_side_effects=True, vmem_limit_bytes=60 * 1024 * 1024
        ),
        name="heads_and_exchanges",
    )(lengths, matching, q, latent, w, g)


def body(queries, latent, w_kv, grad_out, doc_lengths, matching):
    rows = queries.shape[0]
    grad_queries, grad_latent, grad_weight = main_part(doc_lengths, matching, queries, latent, w_kv, grad_out)
    grad_weight = grad_weight.transpose(0, 2, 1, 3).reshape(LATENT // 16, -1)
    return grad_queries, grad_latent.reshape(rows, WIDE), grad_weight


def solution(mesh):
    in_specs = (
        P(("dp", "ctx"), None),
        P(("dp", "ctx"), None),
        P(None, "ctx"),
        P(("dp", "ctx"), None),
        P(),
        P(),
    )
    out_specs = (P(("dp", "ctx"), None), P(("dp", "ctx"), None), P("dp", "ctx"))
    return jax.shard_map(body, mesh=mesh, in_specs=in_specs, out_specs=out_specs, check_vma=False)
```

```python
import jax
import jax.numpy as jnp
from jax import lax
from jax.experimental import pallas as pl
from jax.experimental.pallas import tpu as pltpu
from jax.sharding import PartitionSpec as P

NOPE = 128
ROPE = 64
VDIM = 128
LATENT = 512
HEADS = 64
ROWS = 128
QK = NOPE + ROPE
KV = NOPE + VDIM
WIDE = LATENT + ROPE
MESH = pl.DeviceIdType.MESH
ANY = pl.BlockSpec(memory_space=pl.ANY)
BF = jnp.bfloat16
F32 = jnp.float32
LOW = -1e30


def place():
    dp, ctx = lax.axis_index("dp"), lax.axis_index("ctx")
    return dp // 4, lax.rem(dp, 4), ctx // 2, lax.rem(ctx, 2)


def pick(axis, on_x, on_y):
    return (1 - axis) * on_x + axis * on_y


def wrap(value, n):
    return lax.rem(value + n, n)


def line_dp(axis, position, y, x):
    return pick(axis, 4 * y + position, 4 * position + x)


class Sender:
    def __init__(self):
        self.sent = []
        self.due = []

    def remote(self, src, dst, send_sem, recv_sem, device):
        copy = pltpu.make_async_remote_copy(
            src_ref=src, dst_ref=dst, send_sem=send_sem, recv_sem=recv_sem,
            device_id=device, device_id_type=MESH,
        )
        copy.start()
        self.sent.append(copy)
        return copy

    def local(self, src, dst, sem):
        copy = pltpu.make_async_copy(src, dst, sem)
        copy.start()
        self.due.append(copy)


def signal(device):
    pl.semaphore_signal(pltpu.get_barrier_semaphore(), inc=1, device_id=device, device_id_type=MESH)


def block_at(position, z):
    return lax.rem(position + 8 - z, 4)


def landed(ref, sem):
    pltpu.make_async_copy(ref, ref, sem).wait()


def nt(a, b):
    return lax.dot_general(a, b, (((1,), (1,)), ((), ())), preferred_element_type=F32)


def tn(a, b):
    return lax.dot_general(a, b, (((0,), (0,)), ((), ())), preferred_element_type=F32)


def nn(a, b):
    return jnp.dot(a, b, preferred_element_type=F32)


def heads(t, pair, lo, q, g, lat, w, gq, d_acc, dw_acc, p_t, ds_t):
    rows = q.shape[3]
    block = 2 * rows
    window = 4 * rows
    scale = float(QK) ** -0.5

    nope = lat[t, :, :, :LATENT].reshape(window, LATENT)
    rope = lat[t, :, :, LATENT:].reshape(window, ROPE)
    w_two = w[pair]
    lows = lo[t]
    key_at = lax.broadcasted_iota(jnp.int32, (3 * rows, rows), 0)
    query_at = lax.broadcasted_iota(jnp.int32, (3 * rows, rows), 1)
    kv_two = nn(nope, w_two).astype(BF)
    q_two = q[pair, t].reshape(block, 2 * QK)
    g_two = g[pair, t].reshape(block, 2 * VDIM)
    dq_two, dkv_two = [], []
    d_rope = None
    for h in range(2):
        qh = q_two[:, h * QK:(h + 1) * QK]
        gh = g_two[:, h * VDIM:(h + 1) * VDIM]
        kh = jnp.concatenate([kv_two[:, h * KV:h * KV + NOPE], rope], axis=1)
        vh = kv_two[:, h * KV + NOPE:(h + 1) * KV]
        scores = nt(kh, qh)
        dprobs = nt(vh, gh)
        for s in range(2):
            keys = slice(rows * s, rows * s + 3 * rows)
            queries = slice(rows * s, rows * s + rows)
            low = lows[:, queries] - rows * s
            seen = (key_at >= low) & (key_at <= query_at + block)
            sc = jnp.where(seen, scores[keys, queries] * scale, LOW)
            top = jnp.max(sc, axis=0, keepdims=True)
            ex = jnp.exp(sc - top)
            probs = ex * (1.0 / jnp.sum(ex, axis=0, keepdims=True))
            probs_low = probs.astype(BF)
            dp = dprobs[keys, queries]
            row_dot = jnp.sum(probs_low.astype(F32) * dp, axis=0, keepdims=True)
            p_t[h, keys, queries] = probs_low
            ds_t[h, keys, queries] = (probs * (dp - row_dot)).astype(BF)
        ds = ds_t[h]
        dq_two.append((tn(ds, kh) * scale).astype(BF))
        dk = nn(ds, qh) * scale
        dv = nn(p_t[h], gh)
        d_rope = dk[:, NOPE:] if d_rope is None else d_rope + dk[:, NOPE:]
        dkv_two += [dk[:, :NOPE].astype(BF), dv.astype(BF)]
    gkv = jnp.concatenate(dkv_two, axis=1)
    gq[pair, t] = jnp.concatenate(dq_two, axis=1).reshape(2, rows, 2 * QK)
    d_acc[t, :, :LATENT] += nt(gkv, w_two)
    d_acc[t, :, LATENT:] += d_rope
    dw_acc[...] += tn(nope, gkv)


def main_kernel(
    lengths, matching, q, latent, w, g,
    grad_q, grad_lat, grad_w,
    lo, q_all, g_all, lat_all, w_all, gq, relay, relay_now, chosen, come,
    d_acc, d_halo, d_in, d_line, d_lat, d_sum, d_cross, d_relay, d_pick,
    dw, dw_parts, dw_total, dw_z, dw_last, dw_acc, p_t, ds_t,
    send, recv, l_send, l_recv, w_send, w_recv, w_send2, w_recv2, z_send, z_recv, gq_send, gq_recv,
    d_send, d_recv, c_send, c_recv, a_send, a_recv, b_send, b_recv, r_send, r_recv, out_sem,
    dw_send, dw_recv, dz_send, dz_recv, dl_send, dl_recv,
):
    y, x, z, core = place()
    dp = 4 * y + x
    ctx = 2 * z + core
    mine = pick(core, x, y)
    other = pick(core, y, x)
    before, after = wrap(z - 1, 8), wrap(z + 1, 8)
    rows = q.shape[0]
    block = 2 * rows
    quarter = LATENT // 4
    piece = rows // 4
    two_kv = 2 * KV
    two_q = 2 * QK
    two_v = 2 * VDIM

    w_axis = lax.rem(z, 2)
    w_first = lax.rem(pick(w_axis, x, y) + 4 - z // 2, 4)
    w_other = pick(w_axis, y, x)
    part = block_at(mine, z)
    w_plane = 2 * part + core

    def dw_mate(plane):
        return line_dp(core, lax.rem(part + plane, 4), y, x), 2 * plane + core

    def dw_home(b):
        return 4 * other + z // 2, 2 * w_plane + b

    def dw_source(odd):
        plane = 2 * x + odd
        spot = lax.rem(z // 2 + plane, 4)
        return pick(w_axis, 4 * y + spot, 4 * spot + y), 2 * plane + w_axis

    def is_me(device):
        return (device[0] == dp) & (device[1] == ctx)

    def not_me(device):
        return jnp.logical_not(is_me(device))

    for d in range(16):
        there = lax.rem(dp + d, 16)
        if d:
            signal((there, ctx))
        signal((there, 2 * z + 1 - core))
    signal((dp, 2 * before + core))
    signal((dp, 2 * after + core))
    for d in range(1, 8):
        signal(dw_mate(lax.rem(z + d, 8)))
    strangers = 0
    for b in range(2):
        @pl.when(not_me((dp, 2 * w_plane + b)))
        def _():
            signal((dp, 2 * w_plane + b))

        @pl.when(not_me(dw_source(b)))
        def _():
            signal(dw_source(b))

        strangers += jnp.where(is_me((dp, 2 * (w_first + 4 * b) + w_axis)), 0, 1)
        strangers += jnp.where(is_me(dw_home(b)), 0, 1)

    pl.semaphore_wait(pltpu.get_barrier_semaphore(), 31 + 2 + 7 + strangers)

    moves = Sender()

    def w_home(i):
        return dp, 2 * (w_first + 4 * i) + w_axis

    def w_part(pair, at):
        return w_all.at[pair, pl.ds(pl.multiple_of(at * quarter, quarter), quarter)]

    def w_ends(k):
        src = w.at[pl.ds(pl.multiple_of(w_other * quarter, quarter), quarter), pl.ds(k * two_kv, two_kv)]
        return src, w_part(2 * core + k, w_other)

    def w_copy(k, i):
        src, dst = w_ends(k)
        return pltpu.make_async_remote_copy(
            src_ref=src, dst_ref=dst, send_sem=w_send.at[k, i], recv_sem=w_recv.at[2 * core + k],
            device_id=w_home(i), device_id_type=MESH,
        )

    def send_w(k):
        for i in range(2):
            @pl.when(is_me(w_home(i)))
            def _():
                src, dst = w_ends(k)
                pltpu.make_async_copy(src, dst, w_recv.at[2 * core + k]).start()

            @pl.when(not_me(w_home(i)))
            def _():
                w_copy(k, i).start()

    def share_w(pair):
        landed(w_part(pair, other), w_recv.at[pair])
        for d in range(1, 4):
            target = (line_dp(1 - core, lax.rem(other + d, 4), y, x), 2 * z + core)
            moves.remote(
                w_part(pair, other), w_part(pair, other), w_send2.at[pair, d], w_recv2.at[pair, d], target
            )

    def send_latent(d, e):
        axis = lax.rem(core + e, 2)
        spot = pick(axis, x, y)
        k = 4 * e + d
        dst = lat_all.at[spot, 2 + core]
        if d == 0 and e == 0:
            moves.local(latent, dst, l_recv.at[k])
        else:
            target = (line_dp(axis, lax.rem(spot + d, 4), y, x), 2 * z + axis)
            moves.remote(latent, dst, l_send.at[k], l_recv.at[k], target)

    def rows_ends(kind, pair, d, e):
        axis = lax.rem(core + e, 2)
        spot = pick(axis, x, y)
        there = lax.rem(spot + d, 4)
        target = (line_dp(axis, there, y, x), 2 * z + axis)
        at = 4 * (2 * block_at(there, z) + axis) + pair
        src, width, dst = ((q, two_q, q_all), (g, two_v, g_all))[kind]
        cols = pl.ds(pl.multiple_of(at * width, width), width)
        return src.at[:, cols], dst.at[pair, spot, core], recv.at[kind, pair, 4 * e + d], target

    def rows_copy(kind, pair, d, e):
        src, dst, sem, target = rows_ends(kind, pair, d, e)
        return pltpu.make_async_remote_copy(
            src_ref=src, dst_ref=dst, send_sem=send.at[kind, pair, 4 * e + d], recv_sem=sem,
            device_id=target, device_id_type=MESH,
        )

    def send_rows(pair):
        for d in (0, 1, 3, 2):
            for e in range(2):
                for kind in range(2):
                    if d == 0 and e == 0:
                        src, dst, sem, _ = rows_ends(kind, pair, d, e)
                        pltpu.make_async_copy(src, dst, sem).start()
                    else:
                        rows_copy(kind, pair, d, e).start()

    def forward_latent(d):
        slot = wrap(mine - d, 4)
        for e in range(2):
            landed(lat_all.at[slot, 2 + lax.rem(core + e, 2)], l_recv.at[4 * e + d])
        moves.remote(
            lat_all.at[slot, pl.ds(2, 2)], lat_all.at[slot, pl.ds(0, 2)],
            z_send.at[0, d], z_recv.at[0, d], (dp, 2 * after + core),
        )

    send_w(0)
    for d in (0, 1, 3, 2):
        for e in range(2):
            send_latent(d, e)
    send_w(1)
    send_rows(0)
    d_acc[...] = jnp.zeros_like(d_acc)
    forward_latent(0)
    share_w(0)
    forward_latent(1)
    share_w(2)
    forward_latent(3)
    forward_latent(2)
    send_rows(2)
    share_w(1)
    share_w(3)
    p_t[...] = jnp.zeros_like(p_t)
    ds_t[...] = jnp.zeros_like(ds_t)

    token = z * block + lax.broadcasted_iota(jnp.int32, (1, block), 1)
    for slot in range(4):
        pack = pick(core, 4 * y + slot, 4 * slot + x)
        end = jnp.int32(0)
        begun = jnp.zeros((1, block), jnp.int32)
        for k in range(lengths.shape[1]):
            end = end + lengths[pack, k]
            begun = jnp.where(token >= end, end, begun)
        lo[slot] = begun - (z - 1) * block

    def order(s):
        return s + (s // 2) * (1 - 2 * lax.rem(s, 2))

    def slot_of(s):
        return lax.rem(mine + 4 - order(s), 4)

    def pair_of(i):
        return 2 * lax.rem(i, 2) + i // 2

    def gq_copy(i, there, e, d, half):
        return pltpu.make_async_remote_copy(
            src_ref=gq.at[pair_of(i), :, half, pl.ds(pl.multiple_of(there * piece, piece), piece)],
            dst_ref=relay.at[i, core, pl.ds(4 * other, 4)],
            send_sem=gq_send.at[4 * e + d, i], recv_sem=gq_recv.at[4 * e + d, i],
            device_id=(line_dp(1 - core, there, y, x), 2 * z + half), device_id_type=MESH,
        )

    def relay_pair(i):
        for dm in (2, 1, 3, 0):
            there = lax.rem(other + dm, 4)
            for e in range(2):
                half = lax.rem(core + e, 2)
                if dm == 0 and e == 0:
                    src = gq.at[pair_of(i), :, half, pl.ds(pl.multiple_of(there * piece, piece), piece)]
                    pltpu.make_async_copy(src, relay.at[i, core, pl.ds(4 * other, 4)], gq_recv.at[0, i]).start()
                else:
                    gq_copy(i, there, e, dm, half).start()

    def ahead(d):
        return 4 * lax.rem(y + d // 4, 4) + lax.rem(x + d % 4, 4)

    def behind(d):
        return 4 * wrap(y - d // 4, 4) + wrap(x - d % 4, 4)

    def r_copy(i, d):
        there = ahead(d)
        return pltpu.make_async_remote_copy(
            src_ref=chosen.at[i, there], dst_ref=come.at[i, dp], send_sem=r_send.at[i, d], recv_sem=r_recv.at[i, d],
            device_id=(there, ctx), device_id_type=MESH,
        )

    def deliver(i):
        for k in range(8):
            landed(relay.at[i, core, pl.ds(4 * other, 4)], gq_recv.at[k, i])
        relay_now[...] = relay[i]
        for d in (10, 2, 8, 1, 3, 4, 12, 5, 15, 7, 13, 6, 14, 9, 11, 0):
            there = ahead(d)
            pack = matching[there]
            chosen[i, there, 0] = relay_now[0, pack]
            chosen[i, there, 1] = relay_now[1, 4 * lax.rem(pack, 4) + pack // 4]
            if d == 0:
                pltpu.make_async_copy(chosen.at[i, there], come.at[i, dp], r_recv.at[i, d]).start()
            else:
                r_copy(i, d).start()

    def dw_copy(i, d):
        there = lax.rem(other + d, 4)
        return pltpu.make_async_remote_copy(
            src_ref=dw.at[i, there], dst_ref=dw_parts.at[i, other], send_sem=dw_send.at[i, d],
            recv_sem=dw_recv.at[i, d], device_id=(line_dp(1 - core, there, y, x), 2 * z + core), device_id_type=MESH,
        )

    def weight_first(i):
        dw[i] = dw_acc[lax.rem(i, 2)].astype(BF).reshape(4, quarter, two_kv)
        for d in (2, 1, 3, 0):
            if d == 0:
                pltpu.make_async_copy(dw.at[i, other], dw_parts.at[i, other], dw_recv.at[i, d]).start()
            else:
                dw_copy(i, d).start()

    def dz_copy(i, d):
        there = lax.rem(z + d, 8)
        return pltpu.make_async_remote_copy(
            src_ref=dw_total.at[i, there], dst_ref=dw_z.at[i, z], send_sem=dz_send.at[i, d],
            recv_sem=dz_recv.at[i, d], device_id=dw_mate(there), device_id_type=MESH,
        )

    def weight_second(i):
        for d in range(4):
            landed(dw_parts.at[i, wrap(other - d, 4)], dw_recv.at[i, d])
        total = dw_parts[i, 0].astype(F32)
        for n in range(1, 4):
            total += dw_parts[i, n].astype(F32)
        dw_total[i] = total.astype(BF).reshape(8, quarter // 8, two_kv)
        for d in (4, 3, 5, 2, 6, 1, 7, 0):
            if d == 0:
                pltpu.make_async_copy(dw_total.at[i, z], dw_z.at[i, z], dz_recv.at[i, d]).start()
            else:
                dz_copy(i, d).start()

    odd = lax.rem(z, 2)

    def last_ends(i):
        pair = pair_of(i)
        k = lax.rem(pair, 2)
        return dw_last.at[i], grad_w.at[odd, k], dl_recv.at[odd, k], dw_home(pair // 2)

    def last_copy(i):
        src, dst, sem, home = last_ends(i)
        return pltpu.make_async_remote_copy(
            src_ref=src, dst_ref=dst, send_sem=dl_send.at[i], recv_sem=sem, device_id=home, device_id_type=MESH
        )

    def weight_third(i):
        for d in range(8):
            landed(dw_z.at[i, wrap(z - d, 8)], dz_recv.at[i, d])
        total = dw_z[i, 0].astype(F32)
        for n in range(1, 8):
            total += dw_z[i, n].astype(F32)
        dw_last[i] = total
        src, dst, sem, home = last_ends(i)

        @pl.when(is_me(home))
        def _():
            pltpu.make_async_copy(src, dst, sem).start()

        @pl.when(not_me(home))
        def _():
            last_copy(i).start()

    def halo_copy(s, slot):
        return pltpu.make_async_remote_copy(
            src_ref=d_halo.at[slot], dst_ref=d_in.at[slot], send_sem=z_send.at[1, s], recv_sem=z_recv.at[1, s],
            device_id=(dp, 2 * before + core), device_id_type=MESH,
        )

    def d_copy(s, slot):
        return pltpu.make_async_remote_copy(
            src_ref=d_line.at[slot], dst_ref=d_lat.at[mine], send_sem=d_send.at[s], recv_sem=d_recv.at[s],
            device_id=(line_dp(core, slot, y, x), 2 * z + core), device_id_type=MESH,
        )

    def add_halo(s):
        slot = slot_of(s)
        landed(d_in.at[slot], z_recv.at[1, s])
        d_line[slot] = (d_acc[slot, block:] + d_in[slot].astype(F32)).astype(BF)

        @pl.when(s == 0)
        def _():
            pltpu.make_async_copy(d_line.at[slot], d_lat.at[mine], d_recv.at[s]).start()

        @pl.when(s > 0)
        def _():
            d_copy(s, slot).start()

    def step(n, _):
        early = jnp.where(n < 8, 1, 0)
        i = early * lax.rem(n, 2) + (1 - early) * (n // 4)
        s = early * (n // 2) + (1 - early) * lax.rem(n, 4)
        pair = pair_of(i)
        d = order(s)
        slot = slot_of(s)

        @pl.when(s == 0)
        def _():
            dw_acc[lax.rem(i, 2)] = jnp.zeros(dw_acc.shape[1:], F32)

        @pl.when(s == 0)
        def _():
            for dm in range(1, 4):
                landed(w_part(pair, wrap(other - dm, 4)), w_recv2.at[pair, dm])

        @pl.when(i == 0)
        def _():
            landed(lat_all.at[slot, pl.ds(0, 2)], z_recv.at[0, d])

        for e in range(2):
            half = lax.rem(core + e, 2)
            landed(q_all.at[pair, slot, half], recv.at[0, pair, 4 * e + d])
            landed(g_all.at[pair, slot, half], recv.at[1, pair, 4 * e + d])
        heads(slot, pair, lo, q_all, g_all, lat_all, w_all, gq, d_acc, dw_acc.at[lax.rem(i, 2)], p_t, ds_t)

        for turn, waiting in ((0, 1), (3, 3)):
            @pl.when(n == turn)
            def _():
                send_rows(waiting)

        @pl.when(i == 3)
        def _():
            d_halo[slot] = d_acc[slot, :block].astype(BF)
            halo_copy(s, slot).start()

            @pl.when(s > 0)
            def _():
                add_halo(s - 1)

        @pl.when(s == 3)
        def _():
            relay_pair(i)
            weight_first(i)

        for done, turn in enumerate((11, 13, 15)):
            @pl.when(n == turn)
            def _():
                deliver(jnp.int32(done))
                weight_second(jnp.int32(done))

        for done, turn in enumerate((14, 15)):
            @pl.when(n == turn)
            def _():
                weight_third(jnp.int32(done))

        return 0

    lax.fori_loop(0, 16, step, 0)

    three = jnp.int32(3)
    add_halo(three)

    def collect(s, _):
        landed(d_lat.at[lax.rem(mine + order(s), 4)], d_recv.at[s])
        return 0

    lax.fori_loop(0, 4, collect, 0)
    total = d_lat[0].astype(F32)
    for i in range(1, 4):
        total += d_lat[i].astype(F32)
    d_sum[...] = total.reshape(d_sum.shape)
    moves.remote(d_sum.at[1 - core], d_cross, c_send, c_recv, (dp, 2 * z + 1 - core))
    landed(d_cross, c_recv)
    d_sum[core] += d_cross[...]
    for d in range(16):
        there = ahead(d)
        if d == 0:
            moves.local(d_sum.at[core, there], d_relay.at[dp], a_recv.at[d])
        else:
            moves.remote(d_sum.at[core, there], d_relay.at[dp], a_send.at[d], a_recv.at[d], (there, ctx))
    deliver(three)
    weight_second(three)

    def put(i):
        for d in range(15, -1, -1):
            source = behind(d)
            landed(come.at[i, source], r_recv.at[i, d])
            sy, sx = source // 4, lax.rem(source, 4)
            for j, at, row in ((0, 8 * block_at(sx, z), sy), (1, 8 * block_at(sy, z) + 4, sx)):
                dst = grad_q.at[
                    pl.ds(pl.multiple_of(row * piece, piece), piece),
                    pl.ds(pl.multiple_of((at + pair_of(i)) * two_q, two_q), two_q),
                ]
                pltpu.make_async_copy(come.at[i, source, j], dst, out_sem).start()

    def put_early(i, _):
        put(i)
        return 0

    for d in range(16):
        landed(d_relay.at[dp], a_recv.at[d])
    for d in range(16):
        there = ahead(d)
        d_pick[there] = d_relay[matching[there]]
        if d == 0:
            moves.local(d_pick.at[there], grad_lat.at[dp], b_recv.at[d])
        else:
            moves.remote(d_pick.at[there], grad_lat.at[dp], b_send.at[d], b_recv.at[d], (there, ctx))
    weight_third(jnp.int32(2))
    lax.fori_loop(0, 3, put_early, 0)
    weight_third(three)
    put(three)

    for d in range(16):
        landed(d_pick.at[dp], b_recv.at[d])
    for b in range(2):
        for k in range(2):
            landed(dw_last.at[0], dl_recv.at[b, k])

            @pl.when(not_me(w_home(b)))
            def _():
                w_copy(k, b).wait_send()

    for copy in moves.sent:
        copy.wait_send()

    def rows_left(pair, _):
        for d in range(4):
            for e in range(2):
                if d or e:
                    for kind in range(2):
                        rows_copy(kind, pair, d, e).wait_send()
        return 0

    lax.fori_loop(0, 4, rows_left, 0)

    def close(i, _):
        for k in range(1, 8):
            landed(relay.at[i, core, pl.ds(4 * other, 4)], gq_send.at[k, i])
        for d in range(1, 16):
            r_copy(i, d).wait_send()
        for d in range(1, 4):
            dw_copy(i, d).wait_send()
        for d in range(1, 8):
            dz_copy(i, d).wait_send()

        @pl.when(not_me(dw_home(pair_of(i) // 2)))
        def _():
            last_copy(i).wait_send()

        slot = slot_of(i)
        landed(d_halo.at[slot], z_send.at[1, i])

        @pl.when(i > 0)
        def _():
            landed(d_line.at[slot], d_send.at[i])

        return 0

    lax.fori_loop(0, 4, close, 0)
    landed(grad_q, out_sem)


def main_part(lengths, matching, q, latent, w, g):
    rows = q.shape[0]
    block, window = 2 * rows, 4 * rows
    quarter = LATENT // 4
    two_q, two_v, two_kv = 2 * QK, 2 * VDIM, 2 * KV
    dma = pltpu.SemaphoreType.DMA
    smem = pl.BlockSpec(memory_space=pltpu.SMEM)
    return pl.pallas_call(
        main_kernel,
        out_shape=[
            jax.ShapeDtypeStruct(q.shape, BF),
            jax.ShapeDtypeStruct((16, rows // 16, WIDE), F32),
            jax.ShapeDtypeStruct((2, 2, quarter // 8, two_kv), F32),
        ],
        in_specs=[smem, smem] + [ANY] * 4,
        out_specs=[ANY] * 3,
        scratch_shapes=[
            pltpu.VMEM((4, 1, block), jnp.int32),
            pltpu.VMEM((4, 4, 2, rows, two_q), BF),
            pltpu.VMEM((4, 4, 2, rows, two_v), BF),
            pltpu.VMEM((4, 4, rows, WIDE), BF),
            pltpu.VMEM((4, LATENT, two_kv), BF),
            pltpu.VMEM((4, 4, 2, rows, two_q), BF),
            pltpu.VMEM((4, 2, 16, rows // 4, two_q), BF),
            pltpu.VMEM((2, 16, rows // 4, two_q), BF),
            pltpu.VMEM((4, 16, 2, rows // 4, two_q), BF),
            pltpu.VMEM((4, 16, 2, rows // 4, two_q), BF),
            pltpu.VMEM((4, window, WIDE), F32),
            pltpu.VMEM((4, block, WIDE), BF),
            pltpu.VMEM((4, block, WIDE), BF),
            pltpu.VMEM((4, block, WIDE), BF),
            pltpu.VMEM((4, block, WIDE), BF),
            pltpu.VMEM((2, 16, rows // 16, WIDE), F32),
            pltpu.VMEM((16, rows // 16, WIDE), F32),
            pltpu.VMEM((16, rows // 16, WIDE), F32),
            pltpu.VMEM((16, rows // 16, WIDE), F32),
            pltpu.VMEM((4, 4, quarter, two_kv), BF),
            pltpu.VMEM((4, 4, quarter, two_kv), BF),
            pltpu.VMEM((4, 8, quarter // 8, two_kv), BF),
            pltpu.VMEM((4, 8, quarter // 8, two_kv), BF),
            pltpu.VMEM((4, quarter // 8, two_kv), F32),
            pltpu.VMEM((2, LATENT, two_kv), F32),
            pltpu.VMEM((2, window, block), BF),
            pltpu.VMEM((2, window, block), BF),
            dma((2, 4, 8)), dma((2, 4, 8)), dma((8,)), dma((8,)), dma((2, 2)), dma((4,)), dma((4, 4)), dma((4, 4)),
            dma((2, 4)), dma((2, 4)), dma((8, 4)), dma((8, 4)), dma((4,)), dma((4,)), dma, dma,
            dma((16,)), dma((16,)), dma((16,)), dma((16,)), dma((4, 16)), dma((4, 16)), dma,
            dma((4, 4)), dma((4, 4)), dma((4, 8)), dma((4, 8)), dma((4,)), dma((2, 2)),
        ],
        compiler_params=pltpu.CompilerParams(
            collective_id=0, has_side_effects=True, vmem_limit_bytes=60 * 1024 * 1024
        ),
        name="heads_and_exchanges",
    )(lengths, matching, q, latent, w, g)


def body(queries, latent, w_kv, grad_out, doc_lengths, matching):
    rows = queries.shape[0]
    grad_queries, grad_latent, grad_weight = main_part(doc_lengths, matching, queries, latent, w_kv, grad_out)
    grad_weight = grad_weight.transpose(0, 2, 1, 3).reshape(LATENT // 16, -1)
    return grad_queries, grad_latent.reshape(rows, WIDE), grad_weight


def solution(mesh):
    in_specs = (
        P(("dp", "ctx"), None),
        P(("dp", "ctx"), None),
        P(None, "ctx"),
        P(("dp", "ctx"), None),
        P(),
        P(),
    )
    out_specs = (P(("dp", "ctx"), None), P(("dp", "ctx"), None), P("dp", "ctx"))
    return jax.shard_map(body, mesh=mesh, in_specs=in_specs, out_specs=out_specs, check_vma=False)
```

```python
import jax
import jax.numpy as jnp
from jax import lax
from jax.experimental import pallas as pl
from jax.experimental.pallas import tpu as pltpu
from jax.sharding import PartitionSpec as P

NOPE = 128
ROPE = 64
VDIM = 128
LATENT = 512
HEADS = 64
ROWS = 128
QK = NOPE + ROPE
KV = NOPE + VDIM
WIDE = LATENT + ROPE
MESH = pl.DeviceIdType.MESH
ANY = pl.BlockSpec(memory_space=pl.ANY)
BF = jnp.bfloat16
F32 = jnp.float32
LOW = -1e30


def place():
    dp, ctx = lax.axis_index("dp"), lax.axis_index("ctx")
    return dp // 4, lax.rem(dp, 4), ctx // 2, lax.rem(ctx, 2)


def pick(axis, on_x, on_y):
    return (1 - axis) * on_x + axis * on_y


def wrap(value, n):
    return lax.rem(value + n, n)


def line_dp(axis, position, y, x):
    return pick(axis, 4 * y + position, 4 * position + x)


class Sender:
    def __init__(self):
        self.sent = []
        self.due = []

    def remote(self, src, dst, send_sem, recv_sem, device):
        copy = pltpu.make_async_remote_copy(
            src_ref=src, dst_ref=dst, send_sem=send_sem, recv_sem=recv_sem,
            device_id=device, device_id_type=MESH,
        )
        copy.start()
        self.sent.append(copy)
        return copy

    def local(self, src, dst, sem):
        copy = pltpu.make_async_copy(src, dst, sem)
        copy.start()
        self.due.append(copy)


def signal(device):
    pl.semaphore_signal(pltpu.get_barrier_semaphore(), inc=1, device_id=device, device_id_type=MESH)


def block_at(position, z):
    return lax.rem(position + 8 - z, 4)


def landed(ref, sem):
    pltpu.make_async_copy(ref, ref, sem).wait()


def nt(a, b):
    return lax.dot_general(a, b, (((1,), (1,)), ((), ())), preferred_element_type=F32)


def tn(a, b):
    return lax.dot_general(a, b, (((0,), (0,)), ((), ())), preferred_element_type=F32)


def nn(a, b):
    return jnp.dot(a, b, preferred_element_type=F32)


def heads(t, pair, lo, q, g, lat, w, gq, d_acc, dw_acc, p_t, ds_t):
    rows = q.shape[3]
    block = 2 * rows
    window = 4 * rows
    scale = float(QK) ** -0.5

    nope = lat[t, :, :, :LATENT].reshape(window, LATENT)
    rope = lat[t, :, :, LATENT:].reshape(window, ROPE)
    w_two = w[pair]
    lows = lo[t]
    key_at = lax.broadcasted_iota(jnp.int32, (3 * rows, rows), 0)
    query_at = lax.broadcasted_iota(jnp.int32, (3 * rows, rows), 1)
    kv_two = nn(nope, w_two).astype(BF)
    q_two = q[pair, t].reshape(block, 2 * QK)
    g_two = g[pair, t].reshape(block, 2 * VDIM)
    dq_two, dkv_two = [], []
    d_rope = None
    for h in range(2):
        qh = q_two[:, h * QK:(h + 1) * QK]
        gh = g_two[:, h * VDIM:(h + 1) * VDIM]
        kh = jnp.concatenate([kv_two[:, h * KV:h * KV + NOPE], rope], axis=1)
        vh = kv_two[:, h * KV + NOPE:(h + 1) * KV]
        scores = nt(kh, qh)
        dprobs = nt(vh, gh)
        for s in range(2):
            keys = slice(rows * s, rows * s + 3 * rows)
            queries = slice(rows * s, rows * s + rows)
            low = lows[:, queries] - rows * s
            seen = (key_at >= low) & (key_at <= query_at + block)
            sc = jnp.where(seen, scores[keys, queries] * scale, LOW)
            top = jnp.max(sc, axis=0, keepdims=True)
            ex = jnp.exp(sc - top)
            probs = ex * (1.0 / jnp.sum(ex, axis=0, keepdims=True))
            probs_low = probs.astype(BF)
            dp = dprobs[keys, queries]
            row_dot = jnp.sum(probs_low.astype(F32) * dp, axis=0, keepdims=True)
            p_t[h, keys, queries] = probs_low
            ds_t[h, keys, queries] = (probs * (dp - row_dot)).astype(BF)
        ds = ds_t[h]
        dq_two.append((tn(ds, kh) * scale).astype(BF))
        dk = nn(ds, qh) * scale
        dv = nn(p_t[h], gh)
        d_rope = dk[:, NOPE:] if d_rope is None else d_rope + dk[:, NOPE:]
        dkv_two += [dk[:, :NOPE].astype(BF), dv.astype(BF)]
    gkv = jnp.concatenate(dkv_two, axis=1)
    gq[pair, t] = jnp.concatenate(dq_two, axis=1).reshape(2, rows, 2 * QK)
    d_acc[t, :, :LATENT] += nt(gkv, w_two)
    d_acc[t, :, LATENT:] += d_rope
    dw_acc[...] += tn(nope, gkv)


def main_kernel(
    lengths, matching, q, latent, w, g,
    grad_q, grad_lat, grad_w,
    lo, q_all, g_all, lat_all, w_all, gq, relay, relay_now, chosen, come,
    d_acc, d_halo, d_in, d_line, d_lat, d_sum, d_cross, d_relay, d_pick,
    dw, dw_parts, dw_total, dw_z, dw_last, dw_acc, p_t, ds_t,
    send, recv, l_send, l_recv, w_send, w_recv, w_send2, w_recv2, z_send, z_recv, gq_send, gq_recv,
    d_send, d_recv, c_send, c_recv, a_send, a_recv, b_send, b_recv, r_send, r_recv, out_sem,
    dw_send, dw_recv, dz_send, dz_recv, dl_send, dl_recv,
):
    y, x, z, core = place()
    dp = 4 * y + x
    ctx = 2 * z + core
    mine = pick(core, x, y)
    other = pick(core, y, x)
    before, after = wrap(z - 1, 8), wrap(z + 1, 8)
    rows = q.shape[0]
    block = 2 * rows
    quarter = LATENT // 4
    piece = rows // 4
    two_kv = 2 * KV
    two_q = 2 * QK
    two_v = 2 * VDIM

    w_axis = lax.rem(z, 2)
    w_first = lax.rem(pick(w_axis, x, y) + 4 - z // 2, 4)
    w_other = pick(w_axis, y, x)
    part = block_at(mine, z)
    w_plane = 2 * part + core

    def dw_mate(plane):
        return line_dp(core, lax.rem(part + plane, 4), y, x), 2 * plane + core

    def dw_home(b):
        return 4 * other + z // 2, 2 * w_plane + b

    def dw_source(odd):
        plane = 2 * x + odd
        spot = lax.rem(z // 2 + plane, 4)
        return pick(w_axis, 4 * y + spot, 4 * spot + y), 2 * plane + w_axis

    def is_me(device):
        return (device[0] == dp) & (device[1] == ctx)

    def not_me(device):
        return jnp.logical_not(is_me(device))

    for d in range(16):
        there = lax.rem(dp + d, 16)
        if d:
            signal((there, ctx))
        signal((there, 2 * z + 1 - core))
    signal((dp, 2 * before + core))
    signal((dp, 2 * after + core))
    for d in range(1, 8):
        signal(dw_mate(lax.rem(z + d, 8)))
    strangers = 0
    for b in range(2):
        @pl.when(not_me((dp, 2 * w_plane + b)))
        def _():
            signal((dp, 2 * w_plane + b))

        @pl.when(not_me(dw_source(b)))
        def _():
            signal(dw_source(b))

        strangers += jnp.where(is_me((dp, 2 * (w_first + 4 * b) + w_axis)), 0, 1)
        strangers += jnp.where(is_me(dw_home(b)), 0, 1)

    pl.semaphore_wait(pltpu.get_barrier_semaphore(), 31 + 2 + 7 + strangers)

    moves = Sender()

    def w_home(i):
        return dp, 2 * (w_first + 4 * i) + w_axis

    def w_part(pair, at):
        return w_all.at[pair, pl.ds(pl.multiple_of(at * quarter, quarter), quarter)]

    def w_ends(k):
        src = w.at[pl.ds(pl.multiple_of(w_other * quarter, quarter), quarter), pl.ds(k * two_kv, two_kv)]
        return src, w_part(2 * core + k, w_other)

    def w_copy(k, i):
        src, dst = w_ends(k)
        return pltpu.make_async_remote_copy(
            src_ref=src, dst_ref=dst, send_sem=w_send.at[k, i], recv_sem=w_recv.at[2 * core + k],
            device_id=w_home(i), device_id_type=MESH,
        )

    def send_w(k):
        for i in range(2):
            @pl.when(is_me(w_home(i)))
            def _():
                src, dst = w_ends(k)
                pltpu.make_async_copy(src, dst, w_recv.at[2 * core + k]).start()

            @pl.when(not_me(w_home(i)))
            def _():
                w_copy(k, i).start()

    def share_w(pair):
        landed(w_part(pair, other), w_recv.at[pair])
        for d in range(1, 4):
            target = (line_dp(1 - core, lax.rem(other + d, 4), y, x), 2 * z + core)
            moves.remote(
                w_part(pair, other), w_part(pair, other), w_send2.at[pair, d], w_recv2.at[pair, d], target
            )

    def send_latent(d, e):
        axis = lax.rem(core + e, 2)
        spot = pick(axis, x, y)
        k = 4 * e + d
        dst = lat_all.at[spot, 2 + core]
        if d == 0 and e == 0:
            moves.local(latent, dst, l_recv.at[k])
        else:
            target = (line_dp(axis, lax.rem(spot + d, 4), y, x), 2 * z + axis)
            moves.remote(latent, dst, l_send.at[k], l_recv.at[k], target)

    def rows_ends(kind, pair, d, e):
        axis = lax.rem(core + e, 2)
        spot = pick(axis, x, y)
        there = lax.rem(spot + d, 4)
        target = (line_dp(axis, there, y, x), 2 * z + axis)
        at = 4 * (2 * block_at(there, z) + axis) + pair
        src, width, dst = ((q, two_q, q_all), (g, two_v, g_all))[kind]
        cols = pl.ds(pl.multiple_of(at * width, width), width)
        return src.at[:, cols], dst.at[pair, spot, core], recv.at[kind, pair, 4 * e + d], target

    def rows_copy(kind, pair, d, e):
        src, dst, sem, target = rows_ends(kind, pair, d, e)
        return pltpu.make_async_remote_copy(
            src_ref=src, dst_ref=dst, send_sem=send.at[kind, pair, 4 * e + d], recv_sem=sem,
            device_id=target, device_id_type=MESH,
        )

    def send_rows(pair):
        for d in (0, 1, 3, 2):
            for e in range(2):
                for kind in range(2):
                    if d == 0 and e == 0:
                        src, dst, sem, _ = rows_ends(kind, pair, d, e)
                        pltpu.make_async_copy(src, dst, sem).start()
                    else:
                        rows_copy(kind, pair, d, e).start()

    def forward_latent(d):
        slot = wrap(mine - d, 4)
        for e in range(2):
            landed(lat_all.at[slot, 2 + lax.rem(core + e, 2)], l_recv.at[4 * e + d])
        moves.remote(
            lat_all.at[slot, pl.ds(2, 2)], lat_all.at[slot, pl.ds(0, 2)],
            z_send.at[0, d], z_recv.at[0, d], (dp, 2 * after + core),
        )

    send_w(0)
    for d in (0, 1, 3, 2):
        for e in range(2):
            send_latent(d, e)
    send_w(1)
    send_rows(0)
    d_acc[...] = jnp.zeros_like(d_acc)
    forward_latent(0)
    share_w(0)
    forward_latent(1)
    share_w(2)
    forward_latent(3)
    forward_latent(2)
    send_rows(2)
    share_w(1)
    share_w(3)
    p_t[...] = jnp.zeros_like(p_t)
    ds_t[...] = jnp.zeros_like(ds_t)

    token = z * block + lax.broadcasted_iota(jnp.int32, (1, block), 1)
    for slot in range(4):
        pack = pick(core, 4 * y + slot, 4 * slot + x)
        end = jnp.int32(0)
        begun = jnp.zeros((1, block), jnp.int32)
        for k in range(lengths.shape[1]):
            end = end + lengths[pack, k]
            begun = jnp.where(token >= end, end, begun)
        lo[slot] = begun - (z - 1) * block

    def order(s):
        return s + (s // 2) * (1 - 2 * lax.rem(s, 2))

    def slot_of(s):
        return lax.rem(mine + 4 - order(s), 4)

    def pair_of(i):
        return 2 * lax.rem(i, 2) + i // 2

    def gq_copy(i, there, e, d, half):
        return pltpu.make_async_remote_copy(
            src_ref=gq.at[pair_of(i), :, half, pl.ds(pl.multiple_of(there * piece, piece), piece)],
            dst_ref=relay.at[i, core, pl.ds(4 * other, 4)],
            send_sem=gq_send.at[4 * e + d, i], recv_sem=gq_recv.at[4 * e + d, i],
            device_id=(line_dp(1 - core, there, y, x), 2 * z + half), device_id_type=MESH,
        )

    def relay_pair(i):
        for dm in (2, 1, 3, 0):
            there = lax.rem(other + dm, 4)
            for e in range(2):
                half = lax.rem(core + e, 2)
                if dm == 0 and e == 0:
                    src = gq.at[pair_of(i), :, half, pl.ds(pl.multiple_of(there * piece, piece), piece)]
                    pltpu.make_async_copy(src, relay.at[i, core, pl.ds(4 * other, 4)], gq_recv.at[0, i]).start()
                else:
                    gq_copy(i, there, e, dm, half).start()

    def ahead(d):
        return 4 * lax.rem(y + d // 4, 4) + lax.rem(x + d % 4, 4)

    def behind(d):
        return 4 * wrap(y - d // 4, 4) + wrap(x - d % 4, 4)

    def r_copy(i, d):
        there = ahead(d)
        return pltpu.make_async_remote_copy(
            src_ref=chosen.at[i, there], dst_ref=come.at[i, dp], send_sem=r_send.at[i, d], recv_sem=r_recv.at[i, d],
            device_id=(there, ctx), device_id_type=MESH,
        )

    def deliver(i):
        for k in range(8):
            landed(relay.at[i, core, pl.ds(4 * other, 4)], gq_recv.at[k, i])
        relay_now[...] = relay[i]
        for d in (10, 2, 8, 1, 3, 4, 12, 5, 15, 7, 13, 6, 14, 9, 11, 0):
            there = ahead(d)
            pack = matching[there]
            chosen[i, there, 0] = relay_now[0, pack]
            chosen[i, there, 1] = relay_now[1, 4 * lax.rem(pack, 4) + pack // 4]
            if d == 0:
                pltpu.make_async_copy(chosen.at[i, there], come.at[i, dp], r_recv.at[i, d]).start()
            else:
                r_copy(i, d).start()

    def dw_copy(i, d):
        there = lax.rem(other + d, 4)
        return pltpu.make_async_remote_copy(
            src_ref=dw.at[i, there], dst_ref=dw_parts.at[i, other], send_sem=dw_send.at[i, d],
            recv_sem=dw_recv.at[i, d], device_id=(line_dp(1 - core, there, y, x), 2 * z + core), device_id_type=MESH,
        )

    def weight_first(i):
        dw[i] = dw_acc[lax.rem(i, 2)].astype(BF).reshape(4, quarter, two_kv)
        for d in (2, 1, 3, 0):
            if d == 0:
                pltpu.make_async_copy(dw.at[i, other], dw_parts.at[i, other], dw_recv.at[i, d]).start()
            else:
                dw_copy(i, d).start()

    def dz_copy(i, d):
        there = lax.rem(z + d, 8)
        return pltpu.make_async_remote_copy(
            src_ref=dw_total.at[i, there], dst_ref=dw_z.at[i, z], send_sem=dz_send.at[i, d],
            recv_sem=dz_recv.at[i, d], device_id=dw_mate(there), device_id_type=MESH,
        )

    def weight_second(i):
        for d in range(4):
            landed(dw_parts.at[i, wrap(other - d, 4)], dw_recv.at[i, d])
        total = dw_parts[i, 0].astype(F32)
        for n in range(1, 4):
            total += dw_parts[i, n].astype(F32)
        dw_total[i] = total.astype(BF).reshape(8, quarter // 8, two_kv)
        for d in (4, 3, 5, 2, 6, 1, 7, 0):
            if d == 0:
                pltpu.make_async_copy(dw_total.at[i, z], dw_z.at[i, z], dz_recv.at[i, d]).start()
            else:
                dz_copy(i, d).start()

    odd = lax.rem(z, 2)

    def last_ends(i):
        pair = pair_of(i)
        k = lax.rem(pair, 2)
        return dw_last.at[i], grad_w.at[odd, k], dl_recv.at[odd, k], dw_home(pair // 2)

    def last_copy(i):
        src, dst, sem, home = last_ends(i)
        return pltpu.make_async_remote_copy(
            src_ref=src, dst_ref=dst, send_sem=dl_send.at[i], recv_sem=sem, device_id=home, device_id_type=MESH
        )

    def weight_third(i):
        for d in range(8):
            landed(dw_z.at[i, wrap(z - d, 8)], dz_recv.at[i, d])
        total = dw_z[i, 0].astype(F32)
        for n in range(1, 8):
            total += dw_z[i, n].astype(F32)
        dw_last[i] = total
        src, dst, sem, home = last_ends(i)

        @pl.when(is_me(home))
        def _():
            pltpu.make_async_copy(src, dst, sem).start()

        @pl.when(not_me(home))
        def _():
            last_copy(i).start()

    def halo_copy(s, slot):
        return pltpu.make_async_remote_copy(
            src_ref=d_halo.at[slot], dst_ref=d_in.at[slot], send_sem=z_send.at[1, s], recv_sem=z_recv.at[1, s],
            device_id=(dp, 2 * before + core), device_id_type=MESH,
        )

    def d_copy(s, slot):
        return pltpu.make_async_remote_copy(
            src_ref=d_line.at[slot], dst_ref=d_lat.at[mine], send_sem=d_send.at[s], recv_sem=d_recv.at[s],
            device_id=(line_dp(core, slot, y, x), 2 * z + core), device_id_type=MESH,
        )

    def add_halo(s):
        slot = slot_of(s)
        landed(d_in.at[slot], z_recv.at[1, s])
        d_line[slot] = (d_acc[slot, block:] + d_in[slot].astype(F32)).astype(BF)

        @pl.when(s == 0)
        def _():
            pltpu.make_async_copy(d_line.at[slot], d_lat.at[mine], d_recv.at[s]).start()

        @pl.when(s > 0)
        def _():
            d_copy(s, slot).start()

    def step(n, _):
        early = jnp.where(n < 8, 1, 0)
        i = early * lax.rem(n, 2) + (1 - early) * (n // 4)
        s = early * (n // 2) + (1 - early) * lax.rem(n, 4)
        pair = pair_of(i)
        d = order(s)
        slot = slot_of(s)

        @pl.when(s == 0)
        def _():
            dw_acc[lax.rem(i, 2)] = jnp.zeros(dw_acc.shape[1:], F32)

        @pl.when(s == 0)
        def _():
            for dm in range(1, 4):
                landed(w_part(pair, wrap(other - dm, 4)), w_recv2.at[pair, dm])

        @pl.when(i == 0)
        def _():
            landed(lat_all.at[slot, pl.ds(0, 2)], z_recv.at[0, d])

        for e in range(2):
            half = lax.rem(core + e, 2)
            landed(q_all.at[pair, slot, half], recv.at[0, pair, 4 * e + d])
            landed(g_all.at[pair, slot, half], recv.at[1, pair, 4 * e + d])
        heads(slot, pair, lo, q_all, g_all, lat_all, w_all, gq, d_acc, dw_acc.at[lax.rem(i, 2)], p_t, ds_t)

        for turn, waiting in ((0, 1), (3, 3)):
            @pl.when(n == turn)
            def _():
                send_rows(waiting)

        @pl.when(i == 3)
        def _():
            d_halo[slot] = d_acc[slot, :block].astype(BF)
            halo_copy(s, slot).start()

            @pl.when(s > 0)
            def _():
                add_halo(s - 1)

        @pl.when(s == 3)
        def _():
            weight_first(i)
            relay_pair(i)

        for done, turn in enumerate((11, 13, 15)):
            @pl.when(n == turn)
            def _():
                deliver(jnp.int32(done))
                weight_second(jnp.int32(done))

        for done, turn in enumerate((14, 15)):
            @pl.when(n == turn)
            def _():
                weight_third(jnp.int32(done))

        return 0

    lax.fori_loop(0, 16, step, 0)

    three = jnp.int32(3)
    add_halo(three)

    def collect(s, _):
        landed(d_lat.at[lax.rem(mine + order(s), 4)], d_recv.at[s])
        return 0

    lax.fori_loop(0, 4, collect, 0)
    total = d_lat[0].astype(F32)
    for i in range(1, 4):
        total += d_lat[i].astype(F32)
    d_sum[...] = total.reshape(d_sum.shape)
    moves.remote(d_sum.at[1 - core], d_cross, c_send, c_recv, (dp, 2 * z + 1 - core))
    landed(d_cross, c_recv)
    d_sum[core] += d_cross[...]
    for d in range(16):
        there = ahead(d)
        if d == 0:
            moves.local(d_sum.at[core, there], d_relay.at[dp], a_recv.at[d])
        else:
            moves.remote(d_sum.at[core, there], d_relay.at[dp], a_send.at[d], a_recv.at[d], (there, ctx))
    weight_second(three)
    deliver(three)

    def put(i):
        for d in range(15, -1, -1):
            source = behind(d)
            landed(come.at[i, source], r_recv.at[i, d])
            sy, sx = source // 4, lax.rem(source, 4)
            for j, at, row in ((0, 8 * block_at(sx, z), sy), (1, 8 * block_at(sy, z) + 4, sx)):
                dst = grad_q.at[
                    pl.ds(pl.multiple_of(row * piece, piece), piece),
                    pl.ds(pl.multiple_of((at + pair_of(i)) * two_q, two_q), two_q),
                ]
                pltpu.make_async_copy(come.at[i, source, j], dst, out_sem).start()

    def put_early(i, _):
        put(i)
        return 0

    for d in range(16):
        landed(d_relay.at[dp], a_recv.at[d])
    for d in range(16):
        there = ahead(d)
        d_pick[there] = d_relay[matching[there]]
        if d == 0:
            moves.local(d_pick.at[there], grad_lat.at[dp], b_recv.at[d])
        else:
            moves.remote(d_pick.at[there], grad_lat.at[dp], b_send.at[d], b_recv.at[d], (there, ctx))
    weight_third(jnp.int32(2))
    lax.fori_loop(0, 3, put_early, 0)
    weight_third(three)
    put(three)

    for d in range(16):
        landed(d_pick.at[dp], b_recv.at[d])
    for b in range(2):
        for k in range(2):
            landed(dw_last.at[0], dl_recv.at[b, k])

            @pl.when(not_me(w_home(b)))
            def _():
                w_copy(k, b).wait_send()

    for copy in moves.sent:
        copy.wait_send()

    def rows_left(pair, _):
        for d in range(4):
            for e in range(2):
                if d or e:
                    for kind in range(2):
                        rows_copy(kind, pair, d, e).wait_send()
        return 0

    lax.fori_loop(0, 4, rows_left, 0)

    def close(i, _):
        for k in range(1, 8):
            landed(relay.at[i, core, pl.ds(4 * other, 4)], gq_send.at[k, i])
        for d in range(1, 16):
            r_copy(i, d).wait_send()
        for d in range(1, 4):
            dw_copy(i, d).wait_send()
        for d in range(1, 8):
            dz_copy(i, d).wait_send()

        @pl.when(not_me(dw_home(pair_of(i) // 2)))
        def _():
            last_copy(i).wait_send()

        slot = slot_of(i)
        landed(d_halo.at[slot], z_send.at[1, i])

        @pl.when(i > 0)
        def _():
            landed(d_line.at[slot], d_send.at[i])

        return 0

    lax.fori_loop(0, 4, close, 0)
    landed(grad_q, out_sem)


def main_part(lengths, matching, q, latent, w, g):
    rows = q.shape[0]
    block, window = 2 * rows, 4 * rows
    quarter = LATENT // 4
    two_q, two_v, two_kv = 2 * QK, 2 * VDIM, 2 * KV
    dma = pltpu.SemaphoreType.DMA
    smem = pl.BlockSpec(memory_space=pltpu.SMEM)
    return pl.pallas_call(
        main_kernel,
        out_shape=[
            jax.ShapeDtypeStruct(q.shape, BF),
            jax.ShapeDtypeStruct((16, rows // 16, WIDE), F32),
            jax.ShapeDtypeStruct((2, 2, quarter // 8, two_kv), F32),
        ],
        in_specs=[smem, smem] + [ANY] * 4,
        out_specs=[ANY] * 3,
        scratch_shapes=[
            pltpu.VMEM((4, 1, block), jnp.int32),
            pltpu.VMEM((4, 4, 2, rows, two_q), BF),
            pltpu.VMEM((4, 4, 2, rows, two_v), BF),
            pltpu.VMEM((4, 4, rows, WIDE), BF),
            pltpu.VMEM((4, LATENT, two_kv), BF),
            pltpu.VMEM((4, 4, 2, rows, two_q), BF),
            pltpu.VMEM((4, 2, 16, rows // 4, two_q), BF),
            pltpu.VMEM((2, 16, rows // 4, two_q), BF),
            pltpu.VMEM((4, 16, 2, rows // 4, two_q), BF),
            pltpu.VMEM((4, 16, 2, rows // 4, two_q), BF),
            pltpu.VMEM((4, window, WIDE), F32),
            pltpu.VMEM((4, block, WIDE), BF),
            pltpu.VMEM((4, block, WIDE), BF),
            pltpu.VMEM((4, block, WIDE), BF),
            pltpu.VMEM((4, block, WIDE), BF),
            pltpu.VMEM((2, 16, rows // 16, WIDE), F32),
            pltpu.VMEM((16, rows // 16, WIDE), F32),
            pltpu.VMEM((16, rows // 16, WIDE), F32),
            pltpu.VMEM((16, rows // 16, WIDE), F32),
            pltpu.VMEM((4, 4, quarter, two_kv), BF),
            pltpu.VMEM((4, 4, quarter, two_kv), BF),
            pltpu.VMEM((4, 8, quarter // 8, two_kv), BF),
            pltpu.VMEM((4, 8, quarter // 8, two_kv), BF),
            pltpu.VMEM((4, quarter // 8, two_kv), F32),
            pltpu.VMEM((2, LATENT, two_kv), F32),
            pltpu.VMEM((2, window, block), BF),
            pltpu.VMEM((2, window, block), BF),
            dma((2, 4, 8)), dma((2, 4, 8)), dma((8,)), dma((8,)), dma((2, 2)), dma((4,)), dma((4, 4)), dma((4, 4)),
            dma((2, 4)), dma((2, 4)), dma((8, 4)), dma((8, 4)), dma((4,)), dma((4,)), dma, dma,
            dma((16,)), dma((16,)), dma((16,)), dma((16,)), dma((4, 16)), dma((4, 16)), dma,
            dma((4, 4)), dma((4, 4)), dma((4, 8)), dma((4, 8)), dma((4,)), dma((2, 2)),
        ],
        compiler_params=pltpu.CompilerParams(
            collective_id=0, has_side_effects=True, vmem_limit_bytes=60 * 1024 * 1024
        ),
        name="heads_and_exchanges",
    )(lengths, matching, q, latent, w, g)


def body(queries, latent, w_kv, grad_out, doc_lengths, matching):
    rows = queries.shape[0]
    grad_queries, grad_latent, grad_weight = main_part(doc_lengths, matching, queries, latent, w_kv, grad_out)
    grad_weight = grad_weight.transpose(0, 2, 1, 3).reshape(LATENT // 16, -1)
    return grad_queries, grad_latent.reshape(rows, WIDE), grad_weight


def solution(mesh):
    in_specs = (
        P(("dp", "ctx"), None),
        P(("dp", "ctx"), None),
        P(None, "ctx"),
        P(("dp", "ctx"), None),
        P(),
        P(),
    )
    out_specs = (P(("dp", "ctx"), None), P(("dp", "ctx"), None), P("dp", "ctx"))
    return jax.shard_map(body, mesh=mesh, in_specs=in_specs, out_specs=out_specs, check_vma=False)
```
